512 devices in a mesh: lon: 32 (over y_lo, x, core), lat: 16 (over z, y_hi).
Axes of the slice: x: 4, y: 8 (y_hi: 2, y_lo: 4; y = y_hi * 4 + y_lo), z: 8, core: 2. Of those that a mesh axis runs over, the one named last changes fastest.
Arguments:
- fields: bfloat16 [128, 1024, 256], P('lat', 'lon'), may hold values from -6 to 6
- norm_lon: float32 [256], replicated, may hold values from 0.25 to 1.75
- query_lon: bfloat16 [256, 256], replicated, may hold values from -0.375 to 0.375
- key_lon: bfloat16 [256, 256], replicated, may hold values from -0.375 to 0.375
- value_lon: bfloat16 [256, 256], replicated, may hold values from -0.375 to 0.375
- out_lon: bfloat16 [256, 256], replicated, may hold values from -0.375 to 0.375
- temp_lon: float32 [8], replicated, may hold values from 0.5 to 12
- bias_lon: float32 [8], replicated, may hold values from -2 to 2
- norm_lat: float32 [256], replicated, may hold values from 0.25 to 1.75
- query_lat: bfloat16 [256, 256], replicated, may hold values from -0.375 to 0.375
- key_lat: bfloat16 [256, 256], replicated, may hold values from -0.375 to 0.375
- value_lat: bfloat16 [256, 256], replicated, may hold values from -0.375 to 0.375
- out_lat: bfloat16 [256, 256], replicated, may hold values from -0.375 to 0.375
- temp_lat: float32 [8], replicated, may hold values from 0.5 to 12
- bias_lat: float32 [8], replicated, may hold values from -4 to 0
- norm_mlp: float32 [256], replicated, may hold values from 0.25 to 1.75
- w_gate: bfloat16 [256, 1024], replicated, may hold values from -0.375 to 0.375
- w_up: bfloat16 [256, 1024], replicated, may hold values from -0.375 to 0.375
- w_down: bfloat16 [1024, 256], replicated, may hold values from -0.1875 to 0.1875
Outputs:
- updated: bfloat16 [128, 1024, 256], P('lat', 'lon')
The draws below stay inside these ranges and needn't reach their ends.
All inputs are finite; a program needn't handle non-finite values.
Results may differ from the reference program's by a relative error of at most 0.018.
The reference program's roundings to bfloat16 on the way count: a program that leaves them out, or rounds other values in their place, can miss the bound.
Values may be sent and summed in bfloat16 or wider, within the bound.
No kernel may reach another device: no remote copies, remote signals or barrier semaphores. Data moves between devices by JAX's collectives and lax.ppermute only.
A program may use at most 64 MiB of HBM per device.

```python
import math
import jax
import jax.numpy as jnp
from jax import lax

D = 256
HEADS = 8
FF = 1024
HEAD = 32
LON_DEV = 32
NLON = 1024
NLAT = 128


def block_scale(rng, shape, cuts, least, high):
    def one(dim, parts):
        steps = jax.random.uniform(jax.random.fold_in(jax.random.fold_in(rng, 6), dim), (parts,), jnp.float32, least / len(cuts), high / len(cuts))
        return jnp.repeat(jnp.exp(steps), shape[dim] // parts).reshape((-1,) + (1,) * (len(shape) - dim - 1))

    loudness = one(*cuts[0])
    for cut in cuts[1:]:
        loudness = loudness * one(*cut)
    return loudness


def scatter_about(own_key, extent, scale, reach, shards=(), kind=jnp.bfloat16):
    entries = jax.random.normal(own_key, extent, jnp.float32) * scale
    if len(shards) > 0:
        entries = block_scale(own_key, extent, shards, -0.22, 0.18) * entries
    return jnp.clip(entries, min=-reach, max=reach).astype(kind)


def setup_inputs(seed: int = 0) -> dict:
    seeds = jax.random.split(jax.random.key(seed), 20)
    fields = scatter_about(seeds[0], (NLAT, NLON, D), 1.0, 6.0, ((0, 16), (1, 32)))
    norm_lon = jnp.clip(1.0 + 0.15 * jax.random.normal(seeds[1], (D,), jnp.float32), 0.25, 1.75)
    query_lon = scatter_about(seeds[2], (D, D), D ** -0.5, 0.375)
    key_lon = scatter_about(seeds[3], (D, D), D ** -0.5, 0.375)
    value_lon = scatter_about(seeds[4], (D, D), D ** -0.5, 0.375)
    out_lon = scatter_about(seeds[5], (D, D), D ** -0.5, 0.375)
    temp_lon = jnp.clip(jnp.exp(jax.random.uniform(seeds[6], (HEADS,), jnp.float32, math.log(0.5), math.log(12.0))), 0.5, 12.0)
    bias_lon = jnp.clip(jax.random.uniform(seeds[7], (HEADS,), jnp.float32, -2.0, 2.0), -2.0, 2.0)
    norm_lat = jnp.clip(1.0 + 0.15 * jax.random.normal(seeds[8], (D,), jnp.float32), 0.25, 1.75)
    query_lat = scatter_about(seeds[9], (D, D), D ** -0.5, 0.375)
    key_lat = scatter_about(seeds[10], (D, D), D ** -0.5, 0.375)
    value_lat = scatter_about(seeds[11], (D, D), D ** -0.5, 0.375)
    out_lat = scatter_about(seeds[12], (D, D), D ** -0.5, 0.375)
    temp_lat = jnp.clip(jnp.exp(jax.random.uniform(seeds[13], (HEADS,), jnp.float32, math.log(0.5), math.log(12.0))), 0.5, 12.0)
    bias_lat = jnp.clip(jax.random.uniform(seeds[14], (HEADS,), jnp.float32, -4.0, 0.0), -4.0, 0.0)
    norm_mlp = jnp.clip(1.0 + 0.15 * jax.random.normal(seeds[15], (D,), jnp.float32), 0.25, 1.75)
    w_gate = scatter_about(seeds[16], (D, FF), D ** -0.5, 0.375)
    w_up = scatter_about(seeds[17], (D, FF), D ** -0.5, 0.375)
    w_down = scatter_about(seeds[18], (FF, D), FF ** -0.5, 0.1875)
    return dict(fields=fields, norm_lon=norm_lon, query_lon=query_lon, key_lon=key_lon, value_lon=value_lon, out_lon=out_lon, temp_lon=temp_lon, bias_lon=bias_lon, norm_lat=norm_lat, query_lat=query_lat, key_lat=key_lat, value_lat=value_lat, out_lat=out_lat, temp_lat=temp_lat, bias_lat=bias_lat, norm_mlp=norm_mlp, w_gate=w_gate, w_up=w_up, w_down=w_down)


def normalize(values, gain):
    wide = values.astype(jnp.float32)
    factor = lax.rsqrt(lax.optimization_barrier(jnp.mean(wide * wide, axis=-1, keepdims=True)) + 1e-06)
    return (wide * factor * gain).astype(jnp.bfloat16)

def project(values, weight):
    return jnp.dot(values, weight, preferred_element_type=jnp.float32).astype(jnp.bfloat16)

def attend_lat(queries, keys, values, temp, bias):
    count, cols, depth = queries.shape
    heads = temp.shape[0]
    size = depth // heads
    qh = queries.reshape(count, cols, heads, size).astype(jnp.float32)
    kh = keys.reshape(count, cols, heads, size).astype(jnp.float32)
    vh = values.reshape(count, cols, heads, size).astype(jnp.float32)
    scores = jnp.einsum('ichd,jchd->chij', qh, kh)
    place = jnp.arange(count, dtype=jnp.int32)
    spread = jnp.abs(place[:, None] - place[None, :]).astype(jnp.float32) / count
    scores = scores * (temp / math.sqrt(size))[None, :, None, None] + bias[None, :, None, None] * spread[None, None]
    expo = jnp.exp(scores - lax.optimization_barrier(jnp.max(scores, axis=-1, keepdims=True)))
    denom = lax.optimization_barrier(jnp.sum(expo, axis=-1))
    mixed = jnp.einsum('chij,jchd->ichd', expo.astype(jnp.bfloat16).astype(jnp.float32), vh)
    mixed = mixed / jnp.transpose(denom, (2, 0, 1))[..., None]
    return mixed.astype(jnp.bfloat16).reshape(count, cols, depth)

def reference(fields, norm_lon, query_lon, key_lon, value_lon, out_lon, temp_lon, bias_lon, norm_lat, query_lat, key_lat, value_lat, out_lat, temp_lat, bias_lat, norm_mlp, w_gate, w_up, w_down):
    resid = fields.astype(jnp.float32)
    normed = normalize(resid, norm_lon)
    queries = project(normed, query_lon)
    keys = project(normed, key_lon)
    values = project(normed, value_lon)
    place = jnp.arange(NLON, dtype=jnp.int32)
    angle = (place[:, None] - place[None, :]).astype(jnp.float32) * (2.0 * math.pi / NLON)
    wave = jnp.cos(angle)

    def lon_row(items):
        qr, kr, vr = items
        qh = qr.reshape(NLON, HEADS, HEAD).astype(jnp.float32)
        kh = kr.reshape(NLON, HEADS, HEAD).astype(jnp.float32)
        vh = vr.reshape(NLON, HEADS, HEAD).astype(jnp.float32)
        scores = jnp.einsum('ihd,jhd->hij', qh, kh)
        scores = scores * (temp_lon / math.sqrt(HEAD))[:, None, None] + bias_lon[:, None, None] * wave[None]
        expo = jnp.exp(scores - lax.optimization_barrier(jnp.max(scores, axis=-1, keepdims=True)))
        denom = lax.optimization_barrier(jnp.sum(expo, axis=-1))
        mixed = jnp.einsum('hij,jhd->ihd', expo.astype(jnp.bfloat16).astype(jnp.float32), vh)
        mixed = mixed / jnp.transpose(denom)[..., None]
        return mixed.astype(jnp.bfloat16).reshape(NLON, D)
    attended = lax.map(lon_row, (queries, keys, values))
    first = resid + jnp.dot(attended, out_lon, preferred_element_type=jnp.float32)
    normed_lat = normalize(first, norm_lat)
    blocks = NLON // LON_DEV

    def split(values_in):
        return jnp.transpose(values_in.reshape(NLAT, blocks, LON_DEV, D), (1, 0, 2, 3))
    q2 = split(project(normed_lat, query_lat))
    k2 = split(project(normed_lat, key_lat))
    v2 = split(project(normed_lat, value_lat))
    mixed_lat = lax.map(lambda items: attend_lat(items[0], items[1], items[2], temp_lat, bias_lat), (q2, k2, v2))
    mixed_lat = jnp.transpose(mixed_lat, (1, 0, 2, 3)).reshape(NLAT, NLON, D)
    second = first + jnp.dot(mixed_lat, out_lat, preferred_element_type=jnp.float32)
    normed_mlp = normalize(second, norm_mlp)
    gate = jnp.dot(normed_mlp, w_gate, preferred_element_type=jnp.float32)
    upper = jnp.dot(normed_mlp, w_up, preferred_element_type=jnp.float32)
    hidden = (jax.nn.silu(gate) * upper).astype(jnp.bfloat16)
    return (second + jnp.dot(hidden, w_down, preferred_element_type=jnp.float32)).astype(jnp.bfloat16)
```

```python
import functools
import math

import jax
import jax.numpy as jnp
import numpy as np
from jax import lax
from jax.experimental import pallas as pl
from jax.experimental.pallas import tpu as pltpu
from jax.sharding import Mesh
from jax.sharding import PartitionSpec as P

YL, X, C, Z, YH = 4, 4, 2, 8, 2
HEADS, HEAD, D = 8, 32, 256
F32, BF16 = jnp.float32, jnp.bfloat16
LOG2E = 1.0 / math.log(2.0)
VMEM = pl.BlockSpec(memory_space=pltpu.VMEM)
SMEM = pl.BlockSpec(memory_space=pltpu.SMEM)
PARAMS = pltpu.CompilerParams(vmem_limit_bytes=40 * 1024 * 1024)


def dot(a, b):
    return jnp.dot(a, b, preferred_element_type=F32)


def normed(values, gain):
    factor = lax.rsqrt(jnp.mean(values * values, axis=-1, keepdims=True) + 1e-06)
    return (values * factor * gain).astype(BF16)


def row_kernel(
    yl_ref, ratio_ref, scale_ref, x_ref, gain_ref, wq_ref, wk_ref, wv_ref, wo_ref, keyf_ref, wave_ref,
    out_ref, norm_s, kext_s, att_s, first_s, send_s,
):
    own = pl.ds(pl.multiple_of(yl_ref[0] * 256, 256), 256)
    norm_s[...] = normed(x_ref[...].astype(F32), gain_ref[...])
    keys = dot(norm_s[...], wk_ref[...]).astype(BF16)
    for g in range(2):
        kext_s[g, :, :128] = keys[:, 128 * g : 128 * g + 128]
        kext_s[g, :, 128:] = keyf_ref[...]
    vals_t = dot(norm_s[...], wv_ref[...]).T.astype(BF16)
    qs_t = dot(norm_s[own, :], wq_ref[...]).T.astype(BF16)
    wave = wave_ref[:, own]
    low_rows = lax.broadcasted_iota(jnp.int32, wave.shape, 0) % 3 == 2
    ones = jnp.ones((16, 1024), BF16)
    for h in range(HEADS):
        at = HEAD * (h % 4)
        full = wave * ratio_ref[h]
        high = full.astype(BF16).astype(F32)
        feats = jnp.where(low_rows, full - high, high).astype(BF16)
        parts = [qs_t[HEAD * h : HEAD * h + HEAD], feats, jnp.zeros((112, 256), BF16)]
        if at + HEAD < 128:
            parts.insert(1, jnp.zeros((128 - at - HEAD, 256), BF16))
        if at:
            parts.insert(0, jnp.zeros((at, 256), BF16))
        scores = dot(kext_s[h // 4], jnp.concatenate(parts, axis=0))
        peak = jnp.max(scores, axis=0, keepdims=True)
        expo = jnp.exp2((scores - peak) * scale_ref[h]).astype(BF16)
        mixed = dot(jnp.concatenate([vals_t[HEAD * h : HEAD * h + HEAD], ones], axis=0), expo)
        att_s[HEAD * h : HEAD * h + HEAD, :] = mixed[:HEAD] / mixed[HEAD : HEAD + 1]
    attended = att_s[...].T.astype(BF16)
    first_s[...] = x_ref[own, :].astype(F32) + dot(attended, wo_ref[...])
    for xc in range(8):
        for k in range(4):
            rows = first_s[32 * xc + 8 * k : 32 * xc + 8 * k + 8, :]
            send_s[pl.ds(8 * xc + k, 8, stride=64), :] = rows[:, :128]
            send_s[pl.ds(8 * xc + 4 + k, 8, stride=64), :] = rows[:, 128:]
    sent = send_s[...].astype(BF16)
    out_ref[0] = sent
    out_ref[1] = sent


def col_kernel(
    yh_ref, scale_ref, slope_ref, x_ref, gain_ref, wq_ref, wk_ref, wv_ref, wo_ref, gain2_ref, wg_ref, wu_ref, wd_ref,
    out_ref, wide_s, first_s, norm_s,
):
    wide_s[...] = x_ref[...].astype(F32)
    for k in range(4):
        for f in range(2):
            first_s[k, :, 128 * f : 128 * f + 128] = wide_s[pl.ds(4 * f + k, 128, stride=8), :]
    for k in range(4):
        norm_s[k] = normed(first_s[k], gain_ref[...])
    own = pl.ds(pl.multiple_of(yh_ref[0] * 64, 64), 64)
    flat = norm_s[...].reshape(512, D)
    keys = dot(flat, wk_ref[...]).astype(BF16)
    vals = dot(flat, wv_ref[...]).astype(BF16)
    mine = jnp.concatenate([norm_s[k, own, :] for k in range(4)], axis=0)
    qs = dot(mine, wq_ref[...])
    a = lax.broadcasted_iota(jnp.int32, (64, 128), 0)
    b = lax.broadcasted_iota(jnp.int32, (64, 128), 1)
    lat_a = 16 * (a // 8) + 8 * yh_ref[0] + a % 8
    lat_b = 16 * ((b // 8) % 8) + 8 * (b // 64) + b % 8
    spread = jnp.abs(lat_a - lat_b).astype(F32) * (1.0 / 128)
    head_of = lax.broadcasted_iota(jnp.int32, (64, D), 1) // HEAD
    mixes = []
    for k in range(4):
        q_one = qs[64 * k : 64 * k + 64]
        masked = jnp.concatenate([jnp.where(head_of == h, q_one, 0.0) for h in range(HEADS)], axis=0).astype(BF16)
        raw = lax.dot_general(
            masked, keys[128 * k : 128 * k + 128], (((1,), (1,)), ((), ())), preferred_element_type=F32
        )
        scores = jnp.concatenate(
            [raw[64 * h : 64 * h + 64] * scale_ref[h] + spread * slope_ref[h] for h in range(HEADS)], axis=0
        )
        expo = jnp.exp2(scores - jnp.max(scores, axis=-1, keepdims=True))
        denom = jnp.sum(expo, axis=-1, keepdims=True)
        mixed = dot(expo.astype(BF16), vals[128 * k : 128 * k + 128]) / denom
        total = jnp.where(head_of == 0, mixed[:64], 0.0)
        for h in range(1, HEADS):
            total = jnp.where(head_of == h, mixed[64 * h : 64 * h + 64], total)
        mixes.append(total.astype(BF16))
    resid = jnp.concatenate([first_s[k, own, :] for k in range(4)], axis=0)
    second = resid + dot(jnp.concatenate(mixes, axis=0), wo_ref[...])
    third = normed(second, gain2_ref[...])
    gate = dot(third, wg_ref[...])
    upper = dot(third, wu_ref[...])
    hidden = (gate / (1.0 + jnp.exp(-gate)) * upper).astype(BF16)
    updated = second + dot(hidden, wd_ref[...])
    for k in range(4):
        for z in range(8):
            out_ref[z, k] = updated[64 * k + 8 * z : 64 * k + 8 * z + 8].astype(BF16)


def place_kernel(x_ref, out_ref, wide_s):
    wide_s[0] = x_ref[:, :128].astype(F32)
    wide_s[1] = x_ref[:, 128:].astype(F32)
    for row in range(8):
        parts = []
        for k in range(4):
            at = pl.ds(8 * k + row, 8, stride=32)
            parts.append(jnp.concatenate([wide_s[0, at, :], wide_s[1, at, :]], axis=1))
        out_ref[row] = jnp.concatenate(parts, axis=0).astype(BF16)


def tables():
    angle = np.arange(1024) * (2.0 * math.pi / 1024)
    cos, sin = np.cos(angle), np.sin(angle)
    wave = np.zeros((16, 1024), np.float32)
    wave[0:3], wave[3:6] = cos, sin
    keyf = np.zeros((1024, 128), np.float32)
    for at, v in ((0, cos), (3, sin)):
        high = v.astype(jnp.bfloat16).astype(np.float64)
        keyf[:, at], keyf[:, at + 1], keyf[:, at + 2] = high, v - high, high
    return keyf.astype(jnp.bfloat16), wave


def body(
    fields, norm_lon, query_lon, key_lon, value_lon, out_lon, temp_lon, bias_lon,
    norm_lat, query_lat, key_lat, value_lat, out_lat, temp_lat, bias_lat, norm_mlp, w_gate, w_up, w_down,
):
    keyf, wave = tables()
    yl = lax.axis_index("yl").astype(jnp.int32).reshape(1)
    yh = lax.axis_index("yh").astype(jnp.int32).reshape(1)
    scale_lon = temp_lon / math.sqrt(HEAD)
    scale_lat = temp_lat * (LOG2E / math.sqrt(HEAD))
    row = lax.all_to_all(
        jnp.concatenate([fields] * YL, axis=0), ("yl", "x", "c"), split_axis=0, concat_axis=0, tiled=True
    )
    sent = pl.pallas_call(
        row_kernel,
        out_shape=jax.ShapeDtypeStruct((2, 512, 128), BF16),
        in_specs=[SMEM] * 3 + [VMEM] * 8,
        out_specs=VMEM,
        scratch_shapes=[
            pltpu.VMEM((1024, D), BF16),
            pltpu.VMEM((2, 1024, D), BF16),
            pltpu.VMEM((D, 256), F32),
            pltpu.VMEM((256, D), F32),
            pltpu.VMEM((512, 128), F32),
        ],
        compiler_params=PARAMS,
    )(
        yl, bias_lon / scale_lon, scale_lon * LOG2E, row.reshape(1024, D), norm_lon.reshape(1, D),
        query_lon, key_lon, value_lon, out_lon, keyf, wave,
    )
    cols = lax.all_to_all(
        sent.reshape(128, 8, 128), ("yh", "z", "x", "c"), split_axis=0, concat_axis=0, tiled=True
    )
    done = pl.pallas_call(
        col_kernel,
        out_shape=jax.ShapeDtypeStruct((8, 4, 8, D), BF16),
        in_specs=[SMEM] * 3 + [VMEM] * 10,
        out_specs=VMEM,
        scratch_shapes=[
            pltpu.VMEM((1024, 128), F32),
            pltpu.VMEM((4, 128, D), F32),
            pltpu.VMEM((4, 128, D), BF16),
        ],
        compiler_params=PARAMS,
    )(
        yh, scale_lat, bias_lat * LOG2E, cols.reshape(1024, 128), norm_lat.reshape(1, D),
        query_lat, key_lat, value_lat, out_lat, norm_mlp.reshape(1, D), w_gate, w_up, w_down,
    )
    home = lax.all_to_all(done.reshape(8, 32, D), "z", split_axis=0, concat_axis=0, tiled=True)
    return pl.pallas_call(
        place_kernel,
        out_shape=jax.ShapeDtypeStruct((8, 32, D), BF16),
        in_specs=[VMEM],
        out_specs=VMEM,
        scratch_shapes=[pltpu.VMEM((2, 256, 128), F32)],
        compiler_params=PARAMS,
    )(home.reshape(256, D))


def solution(mesh):
    fine = Mesh(mesh.devices.reshape(YL, X, C, Z, YH), ("yl", "x", "c", "z", "yh"))
    cells = P(("z", "yh"), ("yl", "x", "c"), None)
    return jax.shard_map(body, mesh=fine, in_specs=(cells,) + (P(),) * 18, out_specs=cells, check_vma=False)
```

```python
import functools
import math

import jax
import jax.numpy as jnp
import numpy as np
from jax import lax
from jax.experimental import pallas as pl
from jax.experimental.pallas import tpu as pltpu
from jax.sharding import Mesh
from jax.sharding import PartitionSpec as P

YL, X, C, Z, YH = 4, 4, 2, 8, 2
HEADS, HEAD, D = 8, 32, 256
F32, BF16 = jnp.float32, jnp.bfloat16
LOG2E = 1.0 / math.log(2.0)
VMEM = pl.BlockSpec(memory_space=pltpu.VMEM)
SMEM = pl.BlockSpec(memory_space=pltpu.SMEM)
PARAMS = pltpu.CompilerParams(vmem_limit_bytes=40 * 1024 * 1024)


def dot(a, b):
    return jnp.dot(a, b, preferred_element_type=F32)


def normed(values, gain):
    factor = lax.rsqrt(jnp.mean(values * values, axis=-1, keepdims=True) + 1e-06)
    return (values * factor * gain).astype(BF16)


def prep_kernel(*refs):
    x_ref, gains, heads, (dup_ref, table_ref) = refs[0], refs[1:4], refs[4:8], refs[8:]
    for j in range(YL):
        dup_ref[j] = x_ref[...]
    for j, ref in enumerate(gains):
        table_ref[j : j + 1, :] = ref[...]
    temp_lon, bias_lon, temp_lat, bias_lat = heads
    root = 1.0 / math.sqrt(HEAD)
    for h in range(HEADS):
        rows = [jnp.full((1, D), ref[h], F32) for ref in heads]
        table_ref[8 + h : 9 + h, :] = rows[1] / (rows[0] * root)
        table_ref[16 + h : 17 + h, :] = rows[0] * (root * LOG2E)
        table_ref[24 + h : 25 + h, :] = rows[2] * (root * LOG2E)
        table_ref[32 + h : 33 + h, :] = rows[3] * LOG2E


def row_kernel(
    x_ref, table_ref, wq_ref, wk_ref, wv_ref, wo_ref, keyf_ref, wave_ref,
    out_ref, norm_s, kext_s, att_s, first_s, send_s,
):
    own = pl.ds(pl.multiple_of(lax.axis_index("yl") * 256, 256), 256)
    norm_s[...] = normed(x_ref[...].astype(F32), table_ref[0:1, :])
    keys = dot(norm_s[...], wk_ref[...]).astype(BF16)
    for g in range(2):
        kext_s[g, :, :128] = keys[:, 128 * g : 128 * g + 128]
        kext_s[g, :, 128:] = keyf_ref[...]
    vals_t = dot(norm_s[...], wv_ref[...]).T.astype(BF16)
    qs_t = dot(norm_s[own, :], wq_ref[...]).T.astype(BF16)
    wave = wave_ref[:, own]
    low_rows = lax.broadcasted_iota(jnp.int32, wave.shape, 0) % 3 == 2
    ones = jnp.ones((16, 1024), BF16)

    def scored(h):
        at = HEAD * (h % 4)
        full = wave * table_ref[8 + h : 9 + h, :]
        high = full.astype(BF16).astype(F32)
        feats = jnp.where(low_rows, full - high, high).astype(BF16)
        parts = [qs_t[HEAD * h : HEAD * h + HEAD], feats, jnp.zeros((112, 256), BF16)]
        if at + HEAD < 128:
            parts.insert(1, jnp.zeros((128 - at - HEAD, 256), BF16))
        if at:
            parts.insert(0, jnp.zeros((at, 256), BF16))
        masked = jnp.concatenate(parts, axis=0)
        scores, peak = [], None
        for c in range(0, 1024, 512):
            scores.append(dot(kext_s[h // 4, c : c + 512, :], masked))
            for i in range(0, 512, 128):
                some = scores[-1][i : i + 128]
                peak = some if peak is None else jnp.maximum(peak, some)
        for n in (64, 32, 16, 8):
            peak = jnp.maximum(peak[:n], peak[n : 2 * n])
        return scores, jnp.max(peak, axis=0, keepdims=True)

    def mix(h, expo):
        mixed = dot(jnp.concatenate([vals_t[HEAD * h : HEAD * h + HEAD], ones], axis=0), expo)
        att_s[HEAD * h : HEAD * h + HEAD, :] = mixed[:HEAD] / mixed[HEAD : HEAD + 1]

    ahead, behind = scored(0), None
    for h in range(HEADS):
        scores, peak = ahead
        if h + 1 < HEADS:
            ahead = scored(h + 1)
        scale = table_ref[16 + h : 17 + h, :]
        expo = jnp.concatenate([jnp.exp2((s - peak) * scale).astype(BF16) for s in scores], axis=0)
        if behind is not None:
            mix(h - 1, behind)
        behind = expo
    mix(HEADS - 1, behind)
    attended = att_s[...].T.astype(BF16)
    first_s[...] = x_ref[own, :].astype(F32) + dot(attended, wo_ref[...])
    for xc in range(8):
        for k in range(4):
            rows = first_s[32 * xc + 8 * k : 32 * xc + 8 * k + 8, :]
            send_s[pl.ds(8 * xc + k, 8, stride=64), :] = rows[:, :128]
            send_s[pl.ds(8 * xc + 4 + k, 8, stride=64), :] = rows[:, 128:]
    sent = send_s[...].astype(BF16)
    out_ref[0] = sent
    out_ref[1] = sent


def col_kernel(
    x_ref, table_ref, wq_ref, wk_ref, wv_ref, wo_ref, wg_ref, wu_ref, wd_ref,
    out_ref, wide_s, first_s, norm_s,
):
    wide_s[...] = x_ref[...].astype(F32)
    for k in range(4):
        for f in range(2):
            first_s[k, :, 128 * f : 128 * f + 128] = wide_s[pl.ds(4 * f + k, 128, stride=8), :]
    for k in range(4):
        norm_s[k] = normed(first_s[k], table_ref[1:2, :])
    yh = lax.axis_index("yh")
    own = pl.ds(pl.multiple_of(yh * 64, 64), 64)
    flat = norm_s[...].reshape(512, D)
    keys = dot(flat, wk_ref[...]).astype(BF16)
    vals = dot(flat, wv_ref[...]).astype(BF16)
    mine = jnp.concatenate([norm_s[k, own, :] for k in range(4)], axis=0)
    qs = dot(mine, wq_ref[...])
    a = lax.broadcasted_iota(jnp.int32, (64, 128), 0)
    b = lax.broadcasted_iota(jnp.int32, (64, 128), 1)
    lat_a = 16 * (a // 8) + 8 * yh + a % 8
    lat_b = 16 * ((b // 8) % 8) + 8 * (b // 64) + b % 8
    spread = jnp.abs(lat_a - lat_b).astype(F32) * (1.0 / 128)
    head_of = lax.broadcasted_iota(jnp.int32, (64, D), 1) // HEAD
    mixes = []
    for k in range(4):
        q_one = qs[64 * k : 64 * k + 64]
        masked = jnp.concatenate([jnp.where(head_of == h, q_one, 0.0) for h in range(HEADS)], axis=0).astype(BF16)
        raw = lax.dot_general(
            masked, keys[128 * k : 128 * k + 128], (((1,), (1,)), ((), ())), preferred_element_type=F32
        )
        scores = jnp.concatenate(
            [
                raw[64 * h : 64 * h + 64] * table_ref[24 + h : 25 + h, :128] + spread * table_ref[32 + h : 33 + h, :128]
                for h in range(HEADS)
            ], axis=0
        )
        expo = jnp.exp2(scores - jnp.max(scores, axis=-1, keepdims=True))
        denom = jnp.sum(expo, axis=-1, keepdims=True)
        mixed = dot(expo.astype(BF16), vals[128 * k : 128 * k + 128]) / denom
        total = jnp.where(head_of == 0, mixed[:64], 0.0)
        for h in range(1, HEADS):
            total = jnp.where(head_of == h, mixed[64 * h : 64 * h + 64], total)
        mixes.append(total.astype(BF16))
    resid = jnp.concatenate([first_s[k, own, :] for k in range(4)], axis=0)
    second = resid + dot(jnp.concatenate(mixes, axis=0), wo_ref[...])
    third = normed(second, table_ref[2:3, :])
    gate = dot(third, wg_ref[...])
    upper = dot(third, wu_ref[...])
    hidden = (gate / (1.0 + jnp.exp(-gate)) * upper).astype(BF16)
    updated = second + dot(hidden, wd_ref[...])
    for k in range(4):
        for z in range(8):
            out_ref[z, k] = updated[64 * k + 8 * z : 64 * k + 8 * z + 8].astype(BF16)


def place_kernel(x_ref, out_ref, wide_s):
    wide_s[0] = x_ref[:, :128].astype(F32)
    wide_s[1] = x_ref[:, 128:].astype(F32)
    for row in range(8):
        parts = []
        for k in range(4):
            at = pl.ds(8 * k + row, 8, stride=32)
            parts.append(jnp.concatenate([wide_s[0, at, :], wide_s[1, at, :]], axis=1))
        out_ref[row] = jnp.concatenate(parts, axis=0).astype(BF16)


def tables():
    angle = np.arange(1024) * (2.0 * math.pi / 1024)
    cos, sin = np.cos(angle), np.sin(angle)
    wave = np.zeros((16, 1024), np.float32)
    wave[0:3], wave[3:6] = cos, sin
    keyf = np.zeros((1024, 128), np.float32)
    for at, v in ((0, cos), (3, sin)):
        high = v.astype(jnp.bfloat16).astype(np.float64)
        keyf[:, at], keyf[:, at + 1], keyf[:, at + 2] = high, v - high, high
    return keyf.astype(jnp.bfloat16), wave


def body(
    fields, norm_lon, query_lon, key_lon, value_lon, out_lon, temp_lon, bias_lon,
    norm_lat, query_lat, key_lat, value_lat, out_lat, temp_lat, bias_lat, norm_mlp, w_gate, w_up, w_down,
):
    keyf, wave = tables()
    four, table = pl.pallas_call(
        prep_kernel,
        out_shape=(jax.ShapeDtypeStruct((YL, 8, 32, D), BF16), jax.ShapeDtypeStruct((40, D), F32)),
        in_specs=[VMEM] * 4 + [SMEM] * 4,
        out_specs=(VMEM, VMEM),
        compiler_params=PARAMS,
    )(
        fields, norm_lon.reshape(1, D), norm_lat.reshape(1, D), norm_mlp.reshape(1, D),
        temp_lon, bias_lon, temp_lat, bias_lat,
    )
    row = lax.all_to_all(four.reshape(32, 32, D), ("yl", "x", "c"), split_axis=0, concat_axis=0, tiled=True)
    sent = pl.pallas_call(
        row_kernel,
        out_shape=jax.ShapeDtypeStruct((2, 512, 128), BF16),
        in_specs=[VMEM] * 8,
        out_specs=VMEM,
        scratch_shapes=[
            pltpu.VMEM((1024, D), BF16),
            pltpu.VMEM((2, 1024, D), BF16),
            pltpu.VMEM((D, 256), F32),
            pltpu.VMEM((256, D), F32),
            pltpu.VMEM((512, 128), F32),
        ],
        compiler_params=PARAMS,
    )(
        row.reshape(1024, D), table, query_lon, key_lon, value_lon, out_lon, keyf, wave,
    )
    cols = lax.all_to_all(
        sent.reshape(128, 8, 128), ("yh", "z", "x", "c"), split_axis=0, concat_axis=0, tiled=True
    )
    done = pl.pallas_call(
        col_kernel,
        out_shape=jax.ShapeDtypeStruct((8, 4, 8, D), BF16),
        in_specs=[VMEM] * 9,
        out_specs=VMEM,
        scratch_shapes=[
            pltpu.VMEM((1024, 128), F32),
            pltpu.VMEM((4, 128, D), F32),
            pltpu.VMEM((4, 128, D), BF16),
        ],
        compiler_params=PARAMS,
    )(
        cols.reshape(1024, 128), table, query_lat, key_lat, value_lat, out_lat, w_gate, w_up, w_down,
    )
    home = lax.all_to_all(done.reshape(8, 32, D), "z", split_axis=0, concat_axis=0, tiled=True)
    return pl.pallas_call(
        place_kernel,
        out_shape=jax.ShapeDtypeStruct((8, 32, D), BF16),
        in_specs=[VMEM],
        out_specs=VMEM,
        scratch_shapes=[pltpu.VMEM((2, 256, 128), F32)],
        compiler_params=PARAMS,
    )(home.reshape(256, D))


def solution(mesh):
    fine = Mesh(mesh.devices.reshape(YL, X, C, Z, YH), ("yl", "x", "c", "z", "yh"))
    cells = P(("z", "yh"), ("yl", "x", "c"), None)
    return jax.shard_map(body, mesh=fine, in_specs=(cells,) + (P(),) * 18, out_specs=cells, check_vma=False)
```

```python
import functools
import math

import jax
import jax.numpy as jnp
import numpy as np
from jax import lax
from jax.experimental import pallas as pl
from jax.experimental.pallas import tpu as pltpu
from jax.sharding import Mesh
from jax.sharding import PartitionSpec as P

YA, YB, X, C, Z, YH = 2, 2, 4, 2, 8, 2
HEADS, HEAD, D = 8, 32, 256
F32, BF16 = jnp.float32, jnp.bfloat16
LOG2E = 1.0 / math.log(2.0)
VMEM = pl.BlockSpec(memory_space=pltpu.VMEM)
SMEM = pl.BlockSpec(memory_space=pltpu.SMEM)
PARAMS = pltpu.CompilerParams(vmem_limit_bytes=40 * 1024 * 1024)


def dot(a, b):
    return jnp.dot(a, b, preferred_element_type=F32)


def normed(values, gain):
    factor = lax.rsqrt(jnp.mean(values * values, axis=-1, keepdims=True) + 1e-06)
    return (values * factor * gain).astype(BF16)


def twice_kernel(x_ref, out_ref):
    for j in range(YA):
        out_ref[j] = x_ref[...]


def table_kernel(*refs):
    gains, heads, table_ref = refs[:3], refs[3:7], refs[7]
    for j, ref in enumerate(gains):
        table_ref[j : j + 1, :] = ref[...]
    root = 1.0 / math.sqrt(HEAD)
    for h in range(HEADS):
        rows = [jnp.full((1, D), ref[h], F32) for ref in heads]
        table_ref[8 + h : 9 + h, :] = rows[1] / (rows[0] * root)
        table_ref[16 + h : 17 + h, :] = rows[0] * (root * LOG2E)
        table_ref[24 + h : 25 + h, :] = rows[2] * (root * LOG2E)
        table_ref[32 + h : 33 + h, :] = rows[3] * LOG2E


def row_kernel(
    x_ref, table_ref, wq_ref, wk_ref, wv_ref, wo_ref, keyf_ref, wave_ref,
    out_ref, norm_s, kext_s, att_s, first_s, send_s,
):
    place = 2 * lax.axis_index("c") + lax.axis_index("ya")
    own = pl.ds(pl.multiple_of(place * 256, 256), 256)
    norm_s[...] = normed(x_ref[...].astype(F32), table_ref[0:1, :])
    keys = dot(norm_s[...], wk_ref[...]).astype(BF16)
    for g in range(2):
        kext_s[g, :, :128] = keys[:, 128 * g : 128 * g + 128]
        kext_s[g, :, 128:] = keyf_ref[...]
    vals_t = dot(norm_s[...], wv_ref[...]).T.astype(BF16)
    qs_t = dot(norm_s[own, :], wq_ref[...]).T.astype(BF16)
    wave = wave_ref[:, own]
    low_rows = lax.broadcasted_iota(jnp.int32, wave.shape, 0) % 3 == 2
    ones = jnp.ones((16, 1024), BF16)

    def scored(h):
        at = HEAD * (h % 4)
        full = wave * table_ref[8 + h : 9 + h, :]
        high = full.astype(BF16).astype(F32)
        feats = jnp.where(low_rows, full - high, high).astype(BF16)
        parts = [qs_t[HEAD * h : HEAD * h + HEAD], feats, jnp.zeros((112, 256), BF16)]
        if at + HEAD < 128:
            parts.insert(1, jnp.zeros((128 - at - HEAD, 256), BF16))
        if at:
            parts.insert(0, jnp.zeros((at, 256), BF16))
        masked = jnp.concatenate(parts, axis=0)
        scores, peak = [], None
        for c in range(0, 1024, 512):
            scores.append(dot(kext_s[h // 4, c : c + 512, :], masked))
            for i in range(0, 512, 128):
                some = scores[-1][i : i + 128]
                peak = some if peak is None else jnp.maximum(peak, some)
        for n in (64, 32, 16, 8):
            peak = jnp.maximum(peak[:n], peak[n : 2 * n])
        return scores, jnp.max(peak, axis=0, keepdims=True)

    def mix(h, expo):
        mixed = dot(jnp.concatenate([vals_t[HEAD * h : HEAD * h + HEAD], ones], axis=0), expo)
        att_s[HEAD * h : HEAD * h + HEAD, :] = mixed[:HEAD] / mixed[HEAD : HEAD + 1]

    ahead, behind = scored(0), None
    for h in range(HEADS):
        scores, peak = ahead
        if h + 1 < HEADS:
            ahead = scored(h + 1)
        scale = table_ref[16 + h : 17 + h, :]
        expo = jnp.concatenate([jnp.exp2((s - peak) * scale).astype(BF16) for s in scores], axis=0)
        if behind is not None:
            mix(h - 1, behind)
        behind = expo
    mix(HEADS - 1, behind)
    attended = att_s[...].T.astype(BF16)
    first_s[...] = x_ref[own, :].astype(F32) + dot(attended, wo_ref[...])
    for part in range(8):
        for k in range(4):
            rows = first_s[32 * part + 8 * k : 32 * part + 8 * k + 8, :]
            send_s[pl.ds(8 * part + k, 8, stride=64), :] = rows[:, :128]
            send_s[pl.ds(8 * part + 4 + k, 8, stride=64), :] = rows[:, 128:]
    sent = send_s[...].astype(BF16)
    out_ref[0] = sent
    out_ref[1] = sent


def col_kernel(
    x_ref, table_ref, wq_ref, wk_ref, wv_ref, wo_ref, wg_ref, wu_ref, wd_ref,
    out_ref, wide_s, first_s, norm_s,
):
    wide_s[...] = x_ref[...].astype(F32)
    for k in range(4):
        for f in range(2):
            first_s[k, :, 128 * f : 128 * f + 128] = wide_s[pl.ds(4 * f + k, 128, stride=8), :]
    for k in range(4):
        norm_s[k] = normed(first_s[k], table_ref[1:2, :])
    yh = lax.axis_index("yh")
    own = pl.ds(pl.multiple_of(yh * 64, 64), 64)
    flat = norm_s[...].reshape(512, D)
    keys = dot(flat, wk_ref[...]).astype(BF16)
    vals = dot(flat, wv_ref[...]).astype(BF16)
    mine = jnp.concatenate([norm_s[k, own, :] for k in range(4)], axis=0)
    qs = dot(mine, wq_ref[...])
    a = lax.broadcasted_iota(jnp.int32, (64, 128), 0)
    b = lax.broadcasted_iota(jnp.int32, (64, 128), 1)
    lat_a = 16 * (a // 8) + 8 * yh + a % 8
    lat_b = 16 * ((b // 8) % 8) + 8 * (b // 64) + b % 8
    spread = jnp.abs(lat_a - lat_b).astype(F32) * (1.0 / 128)
    head_of = lax.broadcasted_iota(jnp.int32, (64, D), 1) // HEAD
    mixes = []
    for k in range(4):
        q_one = qs[64 * k : 64 * k + 64]
        masked = jnp.concatenate([jnp.where(head_of == h, q_one, 0.0) for h in range(HEADS)], axis=0).astype(BF16)
        raw = lax.dot_general(
            masked, keys[128 * k : 128 * k + 128], (((1,), (1,)), ((), ())), preferred_element_type=F32
        )
        scores = jnp.concatenate(
            [
                raw[64 * h : 64 * h + 64] * table_ref[24 + h : 25 + h, :128] + spread * table_ref[32 + h : 33 + h, :128]
                for h in range(HEADS)
            ], axis=0
        )
        expo = jnp.exp2(scores - jnp.max(scores, axis=-1, keepdims=True))
        denom = jnp.sum(expo, axis=-1, keepdims=True)
        mixed = dot(expo.astype(BF16), vals[128 * k : 128 * k + 128]) / denom
        total = jnp.where(head_of == 0, mixed[:64], 0.0)
        for h in range(1, HEADS):
            total = jnp.where(head_of == h, mixed[64 * h : 64 * h + 64], total)
        mixes.append(total.astype(BF16))
    resid = jnp.concatenate([first_s[k, own, :] for k in range(4)], axis=0)
    second = resid + dot(jnp.concatenate(mixes, axis=0), wo_ref[...])
    third = normed(second, table_ref[2:3, :])
    gate = dot(third, wg_ref[...])
    upper = dot(third, wu_ref[...])
    hidden = (gate / (1.0 + jnp.exp(-gate)) * upper).astype(BF16)
    updated = second + dot(hidden, wd_ref[...])
    for k in range(4):
        for z in range(8):
            out_ref[z, k] = updated[64 * k + 8 * z : 64 * k + 8 * z + 8].astype(BF16)


def place_kernel(x_ref, out_ref, wide_s):
    wide_s[0] = x_ref[:, :128].astype(F32)
    wide_s[1] = x_ref[:, 128:].astype(F32)
    for row in range(8):
        parts = []
        for k in range(4):
            at = pl.ds(8 * k + row, 8, stride=32)
            parts.append(jnp.concatenate([wide_s[0, at, :], wide_s[1, at, :]], axis=1))
        out_ref[row] = jnp.concatenate(parts, axis=0).astype(BF16)


def tables():
    order = np.arange(1024).reshape(YA * YB * X, C, 32).transpose(1, 0, 2).reshape(1024)
    angle = order * (2.0 * math.pi / 1024)
    cos, sin = np.cos(angle), np.sin(angle)
    wave = np.zeros((16, 1024), np.float32)
    wave[0:3], wave[3:6] = cos, sin
    keyf = np.zeros((1024, 128), np.float32)
    for at, v in ((0, cos), (3, sin)):
        high = v.astype(jnp.bfloat16).astype(np.float64)
        keyf[:, at], keyf[:, at + 1], keyf[:, at + 2] = high, v - high, high
    return keyf.astype(jnp.bfloat16), wave


def body(
    fields, norm_lon, query_lon, key_lon, value_lon, out_lon, temp_lon, bias_lon,
    norm_lat, query_lat, key_lat, value_lat, out_lat, temp_lat, bias_lat, norm_mlp, w_gate, w_up, w_down,
):
    keyf, wave = tables()
    twice = pl.pallas_call(
        twice_kernel,
        out_shape=jax.ShapeDtypeStruct((YA, 8, 32, D), BF16),
        in_specs=[VMEM],
        out_specs=VMEM,
        compiler_params=PARAMS,
    )(fields)
    table = pl.pallas_call(
        table_kernel,
        out_shape=jax.ShapeDtypeStruct((40, D), F32),
        in_specs=[VMEM] * 3 + [SMEM] * 4,
        out_specs=VMEM,
        compiler_params=PARAMS,
    )(
        norm_lon.reshape(1, D), norm_lat.reshape(1, D), norm_mlp.reshape(1, D),
        temp_lon, bias_lon, temp_lat, bias_lat,
    )
    twice, table = lax.optimization_barrier((twice, table))
    half = lax.all_to_all(twice.reshape(16, 32, D), ("ya", "yb", "x"), split_axis=0, concat_axis=0, tiled=True)
    row = lax.all_gather(half, "c", axis=0, tiled=True)
    sent = pl.pallas_call(
        row_kernel,
        out_shape=jax.ShapeDtypeStruct((2, 512, 128), BF16),
        in_specs=[VMEM] * 8,
        out_specs=VMEM,
        scratch_shapes=[
            pltpu.VMEM((1024, D), BF16),
            pltpu.VMEM((2, 1024, D), BF16),
            pltpu.VMEM((D, 256), F32),
            pltpu.VMEM((256, D), F32),
            pltpu.VMEM((512, 128), F32),
        ],
        compiler_params=PARAMS,
    )(
        row.reshape(1024, D), table, query_lon, key_lon, value_lon, out_lon, keyf, wave,
    )
    cols = lax.all_to_all(
        sent.reshape(128, 8, 128), ("yh", "z", "yb", "x"), split_axis=0, concat_axis=0, tiled=True
    )
    done = pl.pallas_call(
        col_kernel,
        out_shape=jax.ShapeDtypeStruct((8, 4, 8, D), BF16),
        in_specs=[VMEM] * 9,
        out_specs=VMEM,
        scratch_shapes=[
            pltpu.VMEM((1024, 128), F32),
            pltpu.VMEM((4, 128, D), F32),
            pltpu.VMEM((4, 128, D), BF16),
        ],
        compiler_params=PARAMS,
    )(
        cols.reshape(1024, 128), table, query_lat, key_lat, value_lat, out_lat, w_gate, w_up, w_down,
    )
    home = lax.all_to_all(done.reshape(8, 32, D), "z", split_axis=0, concat_axis=0, tiled=True)
    return pl.pallas_call(
        place_kernel,
        out_shape=jax.ShapeDtypeStruct((8, 32, D), BF16),
        in_specs=[VMEM],
        out_specs=VMEM,
        scratch_shapes=[pltpu.VMEM((2, 256, 128), F32)],
        compiler_params=PARAMS,
    )(home.reshape(256, D))


def solution(mesh):
    fine = Mesh(mesh.devices.reshape(YA, YB, X, C, Z, YH), ("ya", "yb", "x", "c", "z", "yh"))
    cells = P(("z", "yh"), ("ya", "yb", "x", "c"), None)
    return jax.shard_map(body, mesh=fine, in_specs=(cells,) + (P(),) * 18, out_specs=cells, check_vma=False)
```

```python
import functools
import math

import jax
import jax.numpy as jnp
import numpy as np
from jax import lax
from jax.experimental import pallas as pl
from jax.experimental.pallas import tpu as pltpu
from jax.sharding import Mesh
from jax.sharding import PartitionSpec as P

YL, XA, XB, C, Z, YH = 4, 2, 2, 2, 8, 2
HEADS, HEAD, D = 8, 32, 256
F32, BF16 = jnp.float32, jnp.bfloat16
LOG2E = 1.0 / math.log(2.0)
VMEM = pl.BlockSpec(memory_space=pltpu.VMEM)
PARAMS = pltpu.CompilerParams(vmem_limit_bytes=40 * 1024 * 1024)


def dot(a, b):
    return jnp.dot(a, b, preferred_element_type=F32)


def normed(values, gain):
    factor = lax.rsqrt(jnp.mean(values * values, axis=-1, keepdims=True) + 1e-06)
    return (values * factor * gain).astype(BF16)


def twice_kernel(x_ref, out_ref):
    for j in range(XA):
        out_ref[j] = x_ref[...]


def row_kernel(
    x_ref, table_ref, wq_ref, wk_ref, wv_ref, wo_ref, keyf_ref, wave_ref,
    out_ref, norm_s, kext_s, att_s, first_s, send_s,
):
    place = 2 * lax.axis_index("c") + lax.axis_index("xa")
    own = pl.ds(pl.multiple_of(place * 256, 256), 256)
    norm_s[...] = normed(x_ref[...].astype(F32), table_ref[32:33, :])
    keys = dot(norm_s[...], wk_ref[...]).astype(BF16)
    for g in range(2):
        kext_s[g, :, :128] = keys[:, 128 * g : 128 * g + 128]
        kext_s[g, :, 128:] = keyf_ref[...]
    vals_t = dot(norm_s[...], wv_ref[...]).T.astype(BF16)
    qs_t = dot(norm_s[own, :], wq_ref[...]).T.astype(BF16)
    wave = wave_ref[:, own]
    low_rows = lax.broadcasted_iota(jnp.int32, wave.shape, 0) % 3 == 2
    ones = jnp.ones((16, 1024), BF16)

    def scored(h):
        at = HEAD * (h % 4)
        full = wave * table_ref[h : h + 1, :]
        high = full.astype(BF16).astype(F32)
        feats = jnp.where(low_rows, full - high, high).astype(BF16)
        parts = [qs_t[HEAD * h : HEAD * h + HEAD], feats, jnp.zeros((112, 256), BF16)]
        if at + HEAD < 128:
            parts.insert(1, jnp.zeros((128 - at - HEAD, 256), BF16))
        if at:
            parts.insert(0, jnp.zeros((at, 256), BF16))
        masked = jnp.concatenate(parts, axis=0)
        scores, peak = [], None
        for c in range(0, 1024, 512):
            scores.append(dot(kext_s[h // 4, c : c + 512, :], masked))
            for i in range(0, 512, 128):
                some = scores[-1][i : i + 128]
                peak = some if peak is None else jnp.maximum(peak, some)
        for n in (64, 32, 16, 8):
            peak = jnp.maximum(peak[:n], peak[n : 2 * n])
        return scores, jnp.max(peak, axis=0, keepdims=True)

    def mix(h, expo):
        mixed = dot(jnp.concatenate([vals_t[HEAD * h : HEAD * h + HEAD], ones], axis=0), expo)
        att_s[HEAD * h : HEAD * h + HEAD, :] = mixed[:HEAD] / mixed[HEAD : HEAD + 1]

    ahead, behind = scored(0), None
    for h in range(HEADS):
        scores, peak = ahead
        if h + 1 < HEADS:
            ahead = scored(h + 1)
        scale = table_ref[8 + h : 9 + h, :]
        expo = jnp.concatenate([jnp.exp2((s - peak) * scale).astype(BF16) for s in scores], axis=0)
        if behind is not None:
            mix(h - 1, behind)
        behind = expo
    mix(HEADS - 1, behind)
    attended = att_s[...].T.astype(BF16)
    first_s[...] = x_ref[own, :].astype(F32) + dot(attended, wo_ref[...])
    for part in range(8):
        for k in range(4):
            rows = first_s[32 * part + 8 * k : 32 * part + 8 * k + 8, :]
            send_s[pl.ds(8 * part + k, 8, stride=64), :] = rows[:, :128]
            send_s[pl.ds(8 * part + 4 + k, 8, stride=64), :] = rows[:, 128:]
    sent = send_s[...].astype(BF16)
    out_ref[0] = sent
    out_ref[1] = sent


def col_kernel(
    x_ref, table_ref, wq_ref, wk_ref, wv_ref, wo_ref, wg_ref, wu_ref, wd_ref,
    out_ref, wide_s, first_s, norm_s,
):
    wide_s[...] = x_ref[...].astype(F32)
    for k in range(4):
        for f in range(2):
            first_s[k, :, 128 * f : 128 * f + 128] = wide_s[pl.ds(4 * f + k, 128, stride=8), :]
    for k in range(4):
        norm_s[k] = normed(first_s[k], table_ref[33:34, :])
    yh = lax.axis_index("yh")
    own = pl.ds(pl.multiple_of(yh * 64, 64), 64)
    flat = norm_s[...].reshape(512, D)
    keys = dot(flat, wk_ref[...]).astype(BF16)
    vals = dot(flat, wv_ref[...]).astype(BF16)
    mine = jnp.concatenate([norm_s[k, own, :] for k in range(4)], axis=0)
    qs = dot(mine, wq_ref[...])
    a = lax.broadcasted_iota(jnp.int32, (64, 128), 0)
    b = lax.broadcasted_iota(jnp.int32, (64, 128), 1)
    lat_a = 16 * (a // 8) + 8 * yh + a % 8
    lat_b = 16 * ((b // 8) % 8) + 8 * (b // 64) + b % 8
    spread = jnp.abs(lat_a - lat_b).astype(F32) * (1.0 / 128)
    head_of = lax.broadcasted_iota(jnp.int32, (64, D), 1) // HEAD
    mixes = []
    def scored(k):
        q_one = qs[64 * k : 64 * k + 64]
        masked = jnp.concatenate([jnp.where(head_of == h, q_one, 0.0) for h in range(HEADS)], axis=0).astype(BF16)
        return lax.dot_general(
            masked, keys[128 * k : 128 * k + 128], (((1,), (1,)), ((), ())), preferred_element_type=F32
        )

    bias = jnp.concatenate([spread * table_ref[24 + h : 25 + h, :128] for h in range(HEADS)], axis=0)
    raws = [scored(k) for k in range(4)]
    expos = []
    for k in range(4):
        raw = raws[k]
        scores = bias + jnp.concatenate(
            [raw[64 * h : 64 * h + 64] * table_ref[16 + h : 17 + h, :128] for h in range(HEADS)], axis=0
        )
        expo = jnp.exp2(scores - jnp.max(scores, axis=-1, keepdims=True))
        expos.append((expo.astype(BF16), jnp.sum(expo, axis=-1, keepdims=True)))
    for k in range(4):
        expo, denom = expos[k]
        mixed = dot(expo, vals[128 * k : 128 * k + 128]) / denom
        total = jnp.where(head_of == 0, mixed[:64], 0.0)
        for h in range(1, HEADS):
            total = jnp.where(head_of == h, mixed[64 * h : 64 * h + 64], total)
        mixes.append(total.astype(BF16))
    resid = jnp.concatenate([first_s[k, own, :] for k in range(4)], axis=0)
    second = resid + dot(jnp.concatenate(mixes, axis=0), wo_ref[...])
    third = normed(second, table_ref[34:35, :])
    gate = dot(third, wg_ref[...])
    upper = dot(third, wu_ref[...])
    hidden = (gate / (1.0 + jnp.exp(-gate)) * upper).astype(BF16)
    updated = second + dot(hidden, wd_ref[...])
    for k in range(4):
        for z in range(8):
            out_ref[z, k] = updated[64 * k + 8 * z : 64 * k + 8 * z + 8].astype(BF16)


def place_kernel(x_ref, out_ref, wide_s, done_s, sems):
    wide_s[0] = x_ref[:, :128].astype(F32)
    wide_s[1] = x_ref[:, 128:].astype(F32)
    copies = []
    for row in range(8):
        parts = []
        for k in range(4):
            at = pl.ds(8 * k + row, 8, stride=32)
            parts.append(jnp.concatenate([wide_s[0, at, :], wide_s[1, at, :]], axis=1))
        done_s[row] = jnp.concatenate(parts, axis=0).astype(BF16)
        copies.append(pltpu.make_async_copy(done_s.at[row], out_ref.at[row], sems.at[row]))
        copies[-1].start()
    for copy in copies:
        copy.wait()


def tables():
    order = np.arange(1024).reshape(YL, XA, XB, C, 32).transpose(3, 1, 0, 2, 4).reshape(1024)
    angle = order * (2.0 * math.pi / 1024)
    cos, sin = np.cos(angle), np.sin(angle)
    wave = np.zeros((16, 1024), np.float32)
    wave[0:3], wave[3:6] = cos, sin
    keyf = np.zeros((1024, 128), np.float32)
    for at, v in ((0, cos), (3, sin)):
        high = v.astype(jnp.bfloat16).astype(np.float64)
        keyf[:, at], keyf[:, at + 1], keyf[:, at + 2] = high, v - high, high
    return keyf.astype(jnp.bfloat16), wave


def body(
    fields, norm_lon, query_lon, key_lon, value_lon, out_lon, temp_lon, bias_lon,
    norm_lat, query_lat, key_lat, value_lat, out_lat, temp_lat, bias_lat, norm_mlp, w_gate, w_up, w_down,
):
    keyf, wave = tables()
    twice = pl.pallas_call(
        twice_kernel,
        out_shape=jax.ShapeDtypeStruct((XA, 8, 32, D), BF16),
        in_specs=[VMEM],
        out_specs=VMEM,
        compiler_params=PARAMS,
    )(fields)
    half = lax.all_to_all(twice.reshape(16, 32, D), ("xa", "yl", "xb"), split_axis=0, concat_axis=0, tiled=True)
    row = lax.all_gather(half, "c", axis=0, tiled=True)
    row, temp_lon, bias_lon, temp_lat, bias_lat, norm_lon, norm_lat, norm_mlp = lax.optimization_barrier(
        (row, temp_lon, bias_lon, temp_lat, bias_lat, norm_lon, norm_lat, norm_mlp)
    )
    scale_lon = temp_lon * (1.0 / math.sqrt(HEAD))
    scale_lat = temp_lat * (1.0 / math.sqrt(HEAD))
    values = jnp.stack([bias_lon / scale_lon, scale_lon * LOG2E, scale_lat * LOG2E, bias_lat * LOG2E])
    table = jnp.concatenate(
        [jnp.broadcast_to(values.reshape(32, 1), (32, D)), jnp.stack([norm_lon, norm_lat, norm_mlp])], axis=0
    )
    sent = pl.pallas_call(
        row_kernel,
        out_shape=jax.ShapeDtypeStruct((2, 512, 128), BF16),
        in_specs=[VMEM] * 8,
        out_specs=VMEM,
        scratch_shapes=[
            pltpu.VMEM((1024, D), BF16),
            pltpu.VMEM((2, 1024, D), BF16),
            pltpu.VMEM((D, 256), F32),
            pltpu.VMEM((256, D), F32),
            pltpu.VMEM((512, 128), F32),
        ],
        compiler_params=PARAMS,
    )(
        row.reshape(1024, D), table, query_lon, key_lon, value_lon, out_lon, keyf, wave,
    )
    cols = lax.all_to_all(
        sent.reshape(128, 8, 128), ("yh", "z", "yl", "xb"), split_axis=0, concat_axis=0, tiled=True
    )
    done = pl.pallas_call(
        col_kernel,
        out_shape=jax.ShapeDtypeStruct((8, 4, 8, D), BF16),
        in_specs=[VMEM] * 9,
        out_specs=VMEM,
        scratch_shapes=[
            pltpu.VMEM((1024, 128), F32),
            pltpu.VMEM((4, 128, D), F32),
            pltpu.VMEM((4, 128, D), BF16),
        ],
        compiler_params=PARAMS,
    )(
        cols.reshape(1024, 128), table, query_lat, key_lat, value_lat, out_lat, w_gate, w_up, w_down,
    )
    home = lax.all_to_all(done.reshape(8, 32, D), "z", split_axis=0, concat_axis=0, tiled=True)
    return pl.pallas_call(
        place_kernel,
        out_shape=jax.ShapeDtypeStruct((8, 32, D), BF16),
        in_specs=[VMEM],
        out_specs=pl.BlockSpec(memory_space=pl.ANY),
        scratch_shapes=[pltpu.VMEM((2, 256, 128), F32), pltpu.VMEM((8, 32, D), BF16), pltpu.SemaphoreType.DMA((8,))],
        compiler_params=PARAMS,
    )(home.reshape(256, D))


def solution(mesh):
    fine = Mesh(mesh.devices.reshape(YL, XA, XB, C, Z, YH), ("yl", "xa", "xb", "c", "z", "yh"))
    cells = P(("z", "yh"), ("yl", "xa", "xb", "c"), None)
    return jax.shard_map(body, mesh=fine, in_specs=(cells,) + (P(),) * 18, out_specs=cells, check_vma=False)
```

```python
import functools
import math

import jax
import jax.numpy as jnp
import numpy as np
from jax import lax
from jax.experimental import pallas as pl
from jax.experimental.pallas import tpu as pltpu
from jax.sharding import Mesh
from jax.sharding import PartitionSpec as P

YL, XA, XB, C, Z, YH = 4, 2, 2, 2, 8, 2
HEADS, HEAD, D = 8, 32, 256
F32, BF16 = jnp.float32, jnp.bfloat16
LOG2E = 1.0 / math.log(2.0)
VMEM = pl.BlockSpec(memory_space=pltpu.VMEM)
PARAMS = pltpu.CompilerParams(vmem_limit_bytes=40 * 1024 * 1024)


def dot(a, b):
    return jnp.dot(a, b, preferred_element_type=F32)


def normed(values, gain):
    factor = lax.rsqrt(jnp.mean(values * values, axis=-1, keepdims=True) + 1e-06)
    return (values * factor * gain).astype(BF16)


def twice_kernel(x_ref, out_ref):
    for j in range(XA):
        out_ref[j] = x_ref[...]


def row_kernel(
    x_ref, table_ref, wq_ref, wk_ref, wv_ref, wo_ref, keyf_ref,
    out_ref, norm_s, kext_s, att_s, first_s, send_s,
):
    place = 2 * lax.axis_index("c") + lax.axis_index("xa")
    own = pl.ds(pl.multiple_of(place * 256, 256), 256)
    norm_s[...] = normed(x_ref[...].astype(F32), table_ref[32:33, :])
    keys = dot(norm_s[...], wk_ref[...]).astype(BF16)
    for g in range(2):
        kext_s[g, :, :128] = keys[:, 128 * g : 128 * g + 128]
        kext_s[g, :, 128:] = keyf_ref[...]
    qs_t = dot(norm_s[own, :], wq_ref[...]).astype(BF16).T
    turned = keyf_ref[own, :].astype(F32).T
    at_row = lax.broadcasted_iota(jnp.int32, (16, 256), 0)
    wave = jnp.where(at_row < 3, turned[0:1] + turned[1:2], jnp.where(at_row < 6, turned[3:4] + turned[4:5], 0.0))
    low_rows = at_row % 3 == 2
    ones = jnp.ones((16, 1024), BF16)

    def scored(h):
        at = HEAD * (h % 4)
        full = wave * table_ref[h : h + 1, :]
        high = full.astype(BF16).astype(F32)
        feats = jnp.where(low_rows, full - high, high).astype(BF16)
        parts = [qs_t[HEAD * h : HEAD * h + HEAD], feats, jnp.zeros((112, 256), BF16)]
        if at + HEAD < 128:
            parts.insert(1, jnp.zeros((128 - at - HEAD, 256), BF16))
        if at:
            parts.insert(0, jnp.zeros((at, 256), BF16))
        masked = jnp.concatenate(parts, axis=0)
        scores, peak = [], None
        for c in range(0, 1024, 512):
            scores.append(dot(kext_s[h // 4, c : c + 512, :], masked))
            for i in range(0, 512, 128):
                some = scores[-1][i : i + 128]
                peak = some if peak is None else jnp.maximum(peak, some)
        for n in (64, 32, 16, 8):
            peak = jnp.maximum(peak[:n], peak[n : 2 * n])
        return scores, jnp.max(peak, axis=0, keepdims=True)

    def mix(h, expo):
        mixed = dot(jnp.concatenate([vals_t[HEAD * h : HEAD * h + HEAD], ones], axis=0), expo)
        att_s[HEAD * h : HEAD * h + HEAD, :] = mixed[:HEAD] * (1.0 / mixed[HEAD : HEAD + 1])

    ahead, behind = scored(0), None
    vals_t = dot(norm_s[...], wv_ref[...]).astype(BF16).T
    for h in range(HEADS):
        scores, peak = ahead
        if h + 1 < HEADS:
            ahead = scored(h + 1)
        scale = table_ref[8 + h : 9 + h, :]
        lift = peak * scale
        expo = jnp.concatenate([jnp.exp2(s * scale - lift).astype(BF16) for s in scores], axis=0)
        if behind is not None:
            mix(h - 1, behind)
        behind = expo
    mix(HEADS - 1, behind)
    attended = att_s[...].T.astype(BF16)
    first_s[...] = x_ref[own, :].astype(F32) + dot(attended, wo_ref[...])
    for part in range(8):
        for k in range(4):
            rows = first_s[32 * part + 8 * k : 32 * part + 8 * k + 8, :]
            send_s[pl.ds(8 * part + k, 8, stride=64), :] = rows[:, :128]
            send_s[pl.ds(8 * part + 4 + k, 8, stride=64), :] = rows[:, 128:]
    sent = send_s[...].astype(BF16)
    out_ref[0] = sent
    out_ref[1] = sent


def col_kernel(
    x_ref, table_ref, wq_ref, wk_ref, wv_ref, wo_ref, wg_ref, wu_ref, wd_ref,
    out_ref, wide_s, first_s, norm_s,
):
    wide_s[...] = x_ref[...].astype(F32)
    for k in range(4):
        for f in range(2):
            first_s[k, :, 128 * f : 128 * f + 128] = wide_s[pl.ds(4 * f + k, 128, stride=8), :]
    for k in range(4):
        norm_s[k] = normed(first_s[k], table_ref[33:34, :])
    yh = lax.axis_index("yh")
    own = pl.ds(pl.multiple_of(yh * 64, 64), 64)
    flat = norm_s[...].reshape(512, D)
    keys = dot(flat, wk_ref[...]).astype(BF16)
    vals = dot(flat, wv_ref[...]).astype(BF16)
    mine = jnp.concatenate([norm_s[k, own, :] for k in range(4)], axis=0)
    qs = dot(mine, wq_ref[...])
    a = lax.broadcasted_iota(jnp.int32, (64, 128), 0)
    b = lax.broadcasted_iota(jnp.int32, (64, 128), 1)
    lat_a = 16 * (a // 8) + 8 * yh + a % 8
    lat_b = 16 * ((b // 8) % 8) + 8 * (b // 64) + b % 8
    spread = jnp.abs(lat_a - lat_b).astype(F32) * (1.0 / 128)
    head_of = lax.broadcasted_iota(jnp.int32, (64, D), 1) // HEAD
    mixes = []
    def scored(k):
        q_one = qs[64 * k : 64 * k + 64]
        masked = jnp.concatenate([jnp.where(head_of == h, q_one, 0.0) for h in range(HEADS)], axis=0).astype(BF16)
        return lax.dot_general(
            masked, keys[128 * k : 128 * k + 128], (((1,), (1,)), ((), ())), preferred_element_type=F32
        )

    bias = jnp.concatenate([spread * table_ref[24 + h : 25 + h, :128] for h in range(HEADS)], axis=0)
    raws = [scored(k) for k in range(4)]
    expos = []
    for k in range(4):
        raw = raws[k]
        scores = bias + jnp.concatenate(
            [raw[64 * h : 64 * h + 64] * table_ref[16 + h : 17 + h, :128] for h in range(HEADS)], axis=0
        )
        expo = jnp.exp2(scores - jnp.max(scores, axis=-1, keepdims=True))
        expos.append((expo.astype(BF16), jnp.sum(expo, axis=-1, keepdims=True)))
    for k in range(4):
        expo, denom = expos[k]
        mixed = dot(expo, vals[128 * k : 128 * k + 128]) / denom
        total = jnp.where(head_of == 0, mixed[:64], 0.0)
        for h in range(1, HEADS):
            total = jnp.where(head_of == h, mixed[64 * h : 64 * h + 64], total)
        mixes.append(total.astype(BF16))
    resid = jnp.concatenate([first_s[k, own, :] for k in range(4)], axis=0)
    second = resid + dot(jnp.concatenate(mixes, axis=0), wo_ref[...])
    third = normed(second, table_ref[34:35, :])
    gate = dot(third, wg_ref[...])
    upper = dot(third, wu_ref[...])
    hidden = (gate / (1.0 + jnp.exp(-gate)) * upper).astype(BF16)
    updated = second + dot(hidden, wd_ref[...])
    for k in range(4):
        for z in range(8):
            out_ref[z, k] = updated[64 * k + 8 * z : 64 * k + 8 * z + 8].astype(BF16)


def place_kernel(x_ref, out_ref, wide_s, done_s, sems):
    wide_s[0] = x_ref[:, :128].astype(F32)
    wide_s[1] = x_ref[:, 128:].astype(F32)
    copies = []
    for row in range(8):
        parts = []
        for k in range(4):
            at = pl.ds(8 * k + row, 8, stride=32)
            parts.append(jnp.concatenate([wide_s[0, at, :], wide_s[1, at, :]], axis=1))
        done_s[row] = jnp.concatenate(parts, axis=0).astype(BF16)
        copies.append(pltpu.make_async_copy(done_s.at[row], out_ref.at[row], sems.at[row]))
        copies[-1].start()
    for copy in copies:
        copy.wait()


def key_features():
    order = np.arange(1024).reshape(YL, XA, XB, C, 32).transpose(3, 1, 0, 2, 4).reshape(1024)
    angle = order * (2.0 * math.pi / 1024)
    keyf = np.zeros((1024, 128), np.float32)
    for at, v in ((0, np.cos(angle)), (3, np.sin(angle))):
        high = v.astype(jnp.bfloat16).astype(np.float64)
        keyf[:, at], keyf[:, at + 1], keyf[:, at + 2] = high, v - high, high
    return keyf.astype(jnp.bfloat16)


def body(
    fields, norm_lon, query_lon, key_lon, value_lon, out_lon, temp_lon, bias_lon,
    norm_lat, query_lat, key_lat, value_lat, out_lat, temp_lat, bias_lat, norm_mlp, w_gate, w_up, w_down,
):
    keyf = key_features()
    twice = pl.pallas_call(
        twice_kernel,
        out_shape=jax.ShapeDtypeStruct((XA, 8, 32, D), BF16),
        in_specs=[VMEM],
        out_specs=VMEM,
        compiler_params=PARAMS,
    )(fields)
    half = lax.all_to_all(twice.reshape(16, 32, D), ("xa", "yl", "xb"), split_axis=0, concat_axis=0, tiled=True)
    row = lax.all_gather(half, "c", axis=0, tiled=True)
    row, temp_lon, bias_lon, temp_lat, bias_lat, norm_lon, norm_lat, norm_mlp = lax.optimization_barrier(
        (row, temp_lon, bias_lon, temp_lat, bias_lat, norm_lon, norm_lat, norm_mlp)
    )
    scale_lon = temp_lon * (1.0 / math.sqrt(HEAD))
    scale_lat = temp_lat * (1.0 / math.sqrt(HEAD))
    rows = [bias_lon / scale_lon, scale_lon * LOG2E, scale_lat * LOG2E, bias_lat * LOG2E]
    table = jnp.concatenate(
        [jnp.broadcast_to(r.reshape(HEADS, 1), (HEADS, D)) for r in rows] + [jnp.stack([norm_lon, norm_lat, norm_mlp])], axis=0
    )
    sent = pl.pallas_call(
        row_kernel,
        out_shape=jax.ShapeDtypeStruct((2, 512, 128), BF16),
        in_specs=[VMEM] * 7,
        out_specs=VMEM,
        scratch_shapes=[
            pltpu.VMEM((1024, D), BF16),
            pltpu.VMEM((2, 1024, D), BF16),
            pltpu.VMEM((D, 256), F32),
            pltpu.VMEM((256, D), F32),
            pltpu.VMEM((512, 128), F32),
        ],
        compiler_params=PARAMS,
    )(
        row.reshape(1024, D), table, query_lon, key_lon, value_lon, out_lon, keyf,
    )
    cols = lax.all_to_all(
        sent.reshape(128, 8, 128), ("yh", "z", "yl", "xb"), split_axis=0, concat_axis=0, tiled=True
    )
    done = pl.pallas_call(
        col_kernel,
        out_shape=jax.ShapeDtypeStruct((8, 4, 8, D), BF16),
        in_specs=[VMEM] * 9,
        out_specs=VMEM,
        scratch_shapes=[
            pltpu.VMEM((1024, 128), F32),
            pltpu.VMEM((4, 128, D), F32),
            pltpu.VMEM((4, 128, D), BF16),
        ],
        compiler_params=PARAMS,
    )(
        cols.reshape(1024, 128), table, query_lat, key_lat, value_lat, out_lat, w_gate, w_up, w_down,
    )
    home = lax.all_to_all(done.reshape(8, 32, D), "z", split_axis=0, concat_axis=0, tiled=True)
    return pl.pallas_call(
        place_kernel,
        out_shape=jax.ShapeDtypeStruct((8, 32, D), BF16),
        in_specs=[VMEM],
        out_specs=pl.BlockSpec(memory_space=pl.ANY),
        scratch_shapes=[pltpu.VMEM((2, 256, 128), F32), pltpu.VMEM((8, 32, D), BF16), pltpu.SemaphoreType.DMA((8,))],
        compiler_params=PARAMS,
    )(home.reshape(256, D))


def solution(mesh):
    fine = Mesh(mesh.devices.reshape(YL, XA, XB, C, Z, YH), ("yl", "xa", "xb", "c", "z", "yh"))
    cells = P(("z", "yh"), ("yl", "xa", "xb", "c"), None)
    return jax.shard_map(body, mesh=fine, in_specs=(cells,) + (P(),) * 18, out_specs=cells, check_vma=False)
```

```python
import functools
import math

import jax
import jax.numpy as jnp
import numpy as np
from jax import lax
from jax.experimental import pallas as pl
from jax.experimental.pallas import tpu as pltpu
from jax.sharding import Mesh
from jax.sharding import PartitionSpec as P

YL, XA, XB, C, Z, YH = 4, 2, 2, 2, 8, 2
HEADS, HEAD, D = 8, 32, 256
F32, BF16 = jnp.float32, jnp.bfloat16
LOG2E = 1.0 / math.log(2.0)
VMEM = pl.BlockSpec(memory_space=pltpu.VMEM)
PARAMS = pltpu.CompilerParams(vmem_limit_bytes=40 * 1024 * 1024)


def dot(a, b):
    return jnp.dot(a, b, preferred_element_type=F32)


def normed(values, gain):
    factor = lax.rsqrt(jnp.mean(values * values, axis=-1, keepdims=True) + 1e-06)
    return (values * factor * gain).astype(BF16)


def by_head(ref):
    at = [lax.broadcasted_iota(jnp.int32, (HEADS, HEADS), axis) for axis in range(2)]
    picked = jnp.where(at[0] == at[1], jnp.broadcast_to(ref[...], (HEADS, HEADS)), 0.0)
    return jnp.broadcast_to(jnp.sum(picked, axis=1, keepdims=True), (HEADS, D))


def twice_kernel(x_ref, out_ref):
    for j in range(XA):
        out_ref[j] = x_ref[...]


def row_kernel(
    x_ref, gain_ref, gain2_ref, gain3_ref, temp_ref, bias_ref, temp2_ref, bias2_ref,
    wq_ref, wk_ref, wv_ref, wo_ref, keyf_ref,
    out_ref, next_ref, table_s, norm_s, kext_s, att_s, first_s, send_s,
):
    place = 2 * lax.axis_index("c") + lax.axis_index("xa")
    own = pl.ds(pl.multiple_of(place * 256, 256), 256)
    scales = by_head(temp_ref) * (1.0 / math.sqrt(HEAD))
    table_s[:HEADS] = by_head(bias_ref) / scales
    table_s[HEADS:] = scales * LOG2E
    next_ref[0:8] = by_head(temp2_ref) * (LOG2E / math.sqrt(HEAD))
    next_ref[8:16] = by_head(bias2_ref) * LOG2E
    next_ref[16:17] = gain2_ref[...]
    next_ref[17:18] = gain3_ref[...]
    norm_s[...] = normed(x_ref[...].astype(F32), gain_ref[...])
    keys = dot(norm_s[...], wk_ref[...]).astype(BF16)
    for g in range(2):
        kext_s[g, :, :128] = keys[:, 128 * g : 128 * g + 128]
        kext_s[g, :, 128:] = keyf_ref[...]
    qs_t = dot(norm_s[own, :], wq_ref[...]).astype(BF16).T
    turned = keyf_ref[own, :].astype(F32).T
    at_row = lax.broadcasted_iota(jnp.int32, (16, 256), 0)
    wave = jnp.where(at_row < 3, turned[0:1] + turned[1:2], jnp.where(at_row < 6, turned[3:4] + turned[4:5], 0.0))
    low_rows = at_row % 3 == 2
    ones = jnp.ones((16, 1024), BF16)

    def scored(h):
        at = HEAD * (h % 4)
        full = wave * table_s[h : h + 1, :]
        high = full.astype(BF16).astype(F32)
        feats = jnp.where(low_rows, full - high, high).astype(BF16)
        parts = [qs_t[HEAD * h : HEAD * h + HEAD], feats, jnp.zeros((112, 256), BF16)]
        if at + HEAD < 128:
            parts.insert(1, jnp.zeros((128 - at - HEAD, 256), BF16))
        if at:
            parts.insert(0, jnp.zeros((at, 256), BF16))
        masked = jnp.concatenate(parts, axis=0)
        scores, peak = [], None
        for c in range(0, 1024, 512):
            scores.append(dot(kext_s[h // 4, c : c + 512, :], masked))
            for i in range(0, 512, 128):
                some = scores[-1][i : i + 128]
                peak = some if peak is None else jnp.maximum(peak, some)
        for n in (64, 32, 16, 8):
            peak = jnp.maximum(peak[:n], peak[n : 2 * n])
        return scores, jnp.max(peak, axis=0, keepdims=True)

    def mix(h, expo):
        mixed = dot(jnp.concatenate([vals_t[HEAD * h : HEAD * h + HEAD], ones], axis=0), expo)
        att_s[HEAD * h : HEAD * h + HEAD, :] = mixed[:HEAD] * (1.0 / mixed[HEAD : HEAD + 1])

    ahead, behind = scored(0), None
    vals_t = dot(norm_s[...], wv_ref[...]).astype(BF16).T
    for h in range(HEADS):
        scores, peak = ahead
        if h + 1 < HEADS:
            ahead = scored(h + 1)
        scale = table_s[8 + h : 9 + h, :]
        lift = peak * scale
        expo = jnp.concatenate([jnp.exp2(s * scale - lift).astype(BF16) for s in scores], axis=0)
        if behind is not None:
            mix(h - 1, behind)
        behind = expo
    mix(HEADS - 1, behind)
    attended = att_s[...].T.astype(BF16)
    first_s[...] = x_ref[own, :].astype(F32) + dot(attended, wo_ref[...])
    for part in range(8):
        for k in range(4):
            rows = first_s[32 * part + 8 * k : 32 * part + 8 * k + 8, :]
            send_s[pl.ds(8 * part + k, 8, stride=64), :] = rows[:, :128]
            send_s[pl.ds(8 * part + 4 + k, 8, stride=64), :] = rows[:, 128:]
    sent = send_s[...].astype(BF16)
    out_ref[0] = sent
    out_ref[1] = sent


def col_kernel(
    x_ref, table_ref, wq_ref, wk_ref, wv_ref, wo_ref, wg_ref, wu_ref, wd_ref,
    out_ref, wide_s, first_s, norm_s,
):
    wide_s[...] = x_ref[...].astype(F32)
    for k in range(4):
        for f in range(2):
            first_s[k, :, 128 * f : 128 * f + 128] = wide_s[pl.ds(4 * f + k, 128, stride=8), :]
    for k in range(4):
        norm_s[k] = normed(first_s[k], table_ref[16:17, :])
    yh = lax.axis_index("yh")
    own = pl.ds(pl.multiple_of(yh * 64, 64), 64)
    flat = norm_s[...].reshape(512, D)
    keys = dot(flat, wk_ref[...]).astype(BF16)
    vals = dot(flat, wv_ref[...]).astype(BF16)
    mine = jnp.concatenate([norm_s[k, own, :] for k in range(4)], axis=0)
    qs = dot(mine, wq_ref[...])
    a = lax.broadcasted_iota(jnp.int32, (64, 128), 0)
    b = lax.broadcasted_iota(jnp.int32, (64, 128), 1)
    lat_a = 16 * (a // 8) + 8 * yh + a % 8
    lat_b = 16 * ((b // 8) % 8) + 8 * (b // 64) + b % 8
    spread = jnp.abs(lat_a - lat_b).astype(F32) * (1.0 / 128)
    head_of = lax.broadcasted_iota(jnp.int32, (64, D), 1) // HEAD
    mixes = []
    def scored(k):
        q_one = qs[64 * k : 64 * k + 64]
        masked = jnp.concatenate([jnp.where(head_of == h, q_one, 0.0) for h in range(HEADS)], axis=0).astype(BF16)
        return lax.dot_general(
            masked, keys[128 * k : 128 * k + 128], (((1,), (1,)), ((), ())), preferred_element_type=F32
        )

    bias = jnp.concatenate([spread * table_ref[8 + h : 9 + h, :128] for h in range(HEADS)], axis=0)
    raws = [scored(k) for k in range(4)]
    expos = []
    for k in range(4):
        raw = raws[k]
        scores = bias + jnp.concatenate(
            [raw[64 * h : 64 * h + 64] * table_ref[h : h + 1, :128] for h in range(HEADS)], axis=0
        )
        expo = jnp.exp2(scores - jnp.max(scores, axis=-1, keepdims=True))
        expos.append((expo.astype(BF16), jnp.sum(expo, axis=-1, keepdims=True)))
    for k in range(4):
        expo, denom = expos[k]
        mixed = dot(expo, vals[128 * k : 128 * k + 128]) / denom
        total = jnp.where(head_of == 0, mixed[:64], 0.0)
        for h in range(1, HEADS):
            total = jnp.where(head_of == h, mixed[64 * h : 64 * h + 64], total)
        mixes.append(total.astype(BF16))
    resid = jnp.concatenate([first_s[k, own, :] for k in range(4)], axis=0)
    second = resid + dot(jnp.concatenate(mixes, axis=0), wo_ref[...])
    third = normed(second, table_ref[17:18, :])
    gate = dot(third, wg_ref[...])
    upper = dot(third, wu_ref[...])
    hidden = (gate / (1.0 + jnp.exp(-gate)) * upper).astype(BF16)
    updated = second + dot(hidden, wd_ref[...])
    for k in range(4):
        for z in range(8):
            out_ref[z, k] = updated[64 * k + 8 * z : 64 * k + 8 * z + 8].astype(BF16)


def place_kernel(x_ref, out_ref):
    to = lax.broadcasted_iota(jnp.int32, (256, 256), 0)
    source = 32 * (to % 8) + 8 * ((to // 8) % 4) + to // 32
    moves = jnp.where(lax.broadcasted_iota(jnp.int32, (256, 256), 1) == source, 1.0, 0.0).astype(BF16)
    out_ref[...] = dot(moves, x_ref[...]).astype(BF16).reshape(8, 32, D)


def key_features():
    order = np.arange(1024).reshape(YL, XA, XB, C, 32).transpose(3, 1, 0, 2, 4).reshape(1024)
    angle = order * (2.0 * math.pi / 1024)
    keyf = np.zeros((1024, 128), np.float32)
    for at, v in ((0, np.cos(angle)), (3, np.sin(angle))):
        high = v.astype(jnp.bfloat16).astype(np.float64)
        keyf[:, at], keyf[:, at + 1], keyf[:, at + 2] = high, v - high, high
    return keyf.astype(jnp.bfloat16)


def body(
    fields, norm_lon, query_lon, key_lon, value_lon, out_lon, temp_lon, bias_lon,
    norm_lat, query_lat, key_lat, value_lat, out_lat, temp_lat, bias_lat, norm_mlp, w_gate, w_up, w_down,
):
    keyf = key_features()
    twice = pl.pallas_call(
        twice_kernel,
        out_shape=jax.ShapeDtypeStruct((XA, 8, 32, D), BF16),
        in_specs=[VMEM],
        out_specs=VMEM,
        compiler_params=PARAMS,
    )(fields)
    half = lax.all_to_all(twice.reshape(16, 32, D), ("xa", "yl", "xb"), split_axis=0, concat_axis=0, tiled=True)
    row = lax.all_gather(half, "c", axis=0, tiled=True)
    row = row.reshape(1024, D)
    sent, table = pl.pallas_call(
        row_kernel,
        out_shape=(jax.ShapeDtypeStruct((2, 512, 128), BF16), jax.ShapeDtypeStruct((18, D), F32)),
        in_specs=[VMEM] * 13,
        out_specs=(VMEM, VMEM),
        scratch_shapes=[
            pltpu.VMEM((2 * HEADS, D), F32),
            pltpu.VMEM((1024, D), BF16),
            pltpu.VMEM((2, 1024, D), BF16),
            pltpu.VMEM((D, 256), F32),
            pltpu.VMEM((256, D), F32),
            pltpu.VMEM((512, 128), F32),
        ],
        compiler_params=PARAMS,
    )(
        row, norm_lon.reshape(1, D), norm_lat.reshape(1, D), norm_mlp.reshape(1, D), temp_lon.reshape(1, HEADS),
        bias_lon.reshape(1, HEADS), temp_lat.reshape(1, HEADS), bias_lat.reshape(1, HEADS), query_lon, key_lon, value_lon, out_lon, keyf,
    )
    cols = lax.all_to_all(
        sent.reshape(128, 8, 128), ("yh", "z", "yl", "xb"), split_axis=0, concat_axis=0, tiled=True
    )
    done = pl.pallas_call(
        col_kernel,
        out_shape=jax.ShapeDtypeStruct((8, 4, 8, D), BF16),
        in_specs=[VMEM] * 9,
        out_specs=VMEM,
        scratch_shapes=[
            pltpu.VMEM((1024, 128), F32),
            pltpu.VMEM((4, 128, D), F32),
            pltpu.VMEM((4, 128, D), BF16),
        ],
        compiler_params=PARAMS,
    )(
        cols.reshape(1024, 128), table, query_lat, key_lat, value_lat, out_lat, w_gate, w_up, w_down,
    )
    home = lax.all_to_all(done.reshape(8, 32, D), "z", split_axis=0, concat_axis=0, tiled=True)
    return pl.pallas_call(
        place_kernel,
        out_shape=jax.ShapeDtypeStruct((8, 32, D), BF16),
        in_specs=[VMEM],
        out_specs=VMEM,
        compiler_params=PARAMS,
    )(home.reshape(256, D))


def solution(mesh):
    fine = Mesh(mesh.devices.reshape(YL, XA, XB, C, Z, YH), ("yl", "xa", "xb", "c", "z", "yh"))
    cells = P(("z", "yh"), ("yl", "xa", "xb", "c"), None)
    return jax.shard_map(body, mesh=fine, in_specs=(cells,) + (P(),) * 18, out_specs=cells, check_vma=False)
```

```python
import functools
import math

import jax
import jax.numpy as jnp
import numpy as np
from jax import lax
from jax.experimental import pallas as pl
from jax.experimental.pallas import tpu as pltpu
from jax.sharding import Mesh
from jax.sharding import PartitionSpec as P

YL, XA, XB, C, Z, YH = 4, 2, 2, 2, 8, 2
HEADS, HEAD, D = 8, 32, 256
F32, BF16 = jnp.float32, jnp.bfloat16
LOG2E = 1.0 / math.log(2.0)
VMEM = pl.BlockSpec(memory_space=pltpu.VMEM)
PARAMS = pltpu.CompilerParams(vmem_limit_bytes=40 * 1024 * 1024)


def dot(a, b):
    return jnp.dot(a, b, preferred_element_type=F32)


def normed(values, gain):
    factor = lax.rsqrt(jnp.mean(values * values, axis=-1, keepdims=True) + 1e-06)
    return (values * factor * gain).astype(BF16)


def by_head(ref):
    at = [lax.broadcasted_iota(jnp.int32, (HEADS, HEADS), axis) for axis in range(2)]
    picked = jnp.where(at[0] == at[1], jnp.broadcast_to(ref[...], (HEADS, HEADS)), 0.0)
    return jnp.broadcast_to(jnp.sum(picked, axis=1, keepdims=True), (HEADS, D))


def twice_kernel(x_ref, out_ref):
    for j in range(XA):
        out_ref[j] = x_ref[...]


def row_kernel(
    x_ref, gain_ref, gain2_ref, gain3_ref, temp_ref, bias_ref, temp2_ref, bias2_ref,
    wq_ref, wk_ref, wv_ref, wo_ref, keyf_ref,
    out_ref, next_ref, table_s, norm_s, kext_s, att_s, first_s, send_s,
):
    place = 2 * lax.axis_index("c") + lax.axis_index("xa")
    own = pl.ds(pl.multiple_of(place * 256, 256), 256)
    scales = by_head(temp_ref) * (1.0 / math.sqrt(HEAD))
    table_s[:HEADS] = by_head(bias_ref) / scales
    table_s[HEADS:] = scales * LOG2E
    next_ref[0:8] = by_head(temp2_ref) * (LOG2E / math.sqrt(HEAD))
    next_ref[8:16] = by_head(bias2_ref) * LOG2E
    next_ref[16:17] = gain2_ref[...]
    next_ref[17:18] = gain3_ref[...]
    norm_s[...] = normed(x_ref[...].astype(F32), gain_ref[...])
    keys = dot(norm_s[...], wk_ref[...]).astype(BF16)
    for g in range(2):
        kext_s[g, :, :128] = keys[:, 128 * g : 128 * g + 128]
        kext_s[g, :, 128:] = keyf_ref[...]
    qs_t = dot(norm_s[own, :], wq_ref[...]).astype(BF16).T
    turned = keyf_ref[own, :].astype(F32).T
    at_row = lax.broadcasted_iota(jnp.int32, (16, 256), 0)
    wave = jnp.where(at_row < 3, turned[0:1] + turned[1:2], jnp.where(at_row < 6, turned[3:4] + turned[4:5], 0.0))
    low_rows = at_row % 3 == 2
    ones = jnp.ones((16, 1024), BF16)

    def scored(h):
        at = HEAD * (h % 4)
        full = wave * table_s[h : h + 1, :]
        high = full.astype(BF16).astype(F32)
        feats = jnp.where(low_rows, full - high, high).astype(BF16)
        parts = [qs_t[HEAD * h : HEAD * h + HEAD], feats, jnp.zeros((112, 256), BF16)]
        if at + HEAD < 128:
            parts.insert(1, jnp.zeros((128 - at - HEAD, 256), BF16))
        if at:
            parts.insert(0, jnp.zeros((at, 256), BF16))
        masked = jnp.concatenate(parts, axis=0)
        scores, peak = [], None
        for c in range(0, 1024, 512):
            scores.append(dot(kext_s[h // 4, c : c + 512, :], masked))
            for i in range(0, 512, 128):
                some = scores[-1][i : i + 128]
                peak = some if peak is None else jnp.maximum(peak, some)
        for n in (64, 32, 16, 8):
            peak = jnp.maximum(peak[:n], peak[n : 2 * n])
        return scores, jnp.max(peak, axis=0, keepdims=True)

    def mix(h, expo):
        mixed = dot(jnp.concatenate([vals_t[HEAD * h : HEAD * h + HEAD], ones], axis=0), expo)
        att_s[HEAD * h : HEAD * h + HEAD, :] = mixed[:HEAD] * (1.0 / mixed[HEAD : HEAD + 1])

    ahead, behind = scored(0), None
    vals_t = dot(norm_s[...], wv_ref[...]).astype(BF16).T
    for h in range(HEADS):
        scores, peak = ahead
        if h + 1 < HEADS:
            ahead = scored(h + 1)
        scale = table_s[8 + h : 9 + h, :]
        lift = peak * scale
        expo = jnp.concatenate([jnp.exp2(s * scale - lift).astype(BF16) for s in scores], axis=0)
        if behind is not None:
            mix(h - 1, behind)
        behind = expo
    mix(HEADS - 1, behind)
    attended = att_s[...].T.astype(BF16)
    first_s[...] = x_ref[own, :].astype(F32) + dot(attended, wo_ref[...])
    for part in range(8):
        for k in range(4):
            rows = first_s[32 * part + 8 * k : 32 * part + 8 * k + 8, :]
            send_s[pl.ds(8 * part + k, 8, stride=64), :] = rows[:, :128]
            send_s[pl.ds(8 * part + 4 + k, 8, stride=64), :] = rows[:, 128:]
    sent = send_s[...].astype(BF16)
    out_ref[0] = sent
    out_ref[1] = sent


def col_kernel(
    x_ref, table_ref, wq_ref, wk_ref, wv_ref, wo_ref, wg_ref, wu_ref, wd_ref,
    out_ref, wide_s, first_s, norm_s,
):
    wide_s[...] = x_ref[...].astype(F32)
    for k in range(4):
        for f in range(2):
            first_s[k, :, 128 * f : 128 * f + 128] = wide_s[pl.ds(4 * f + k, 128, stride=8), :]
    for k in range(4):
        norm_s[k] = normed(first_s[k], table_ref[16:17, :])
    yh = lax.axis_index("yh")
    own = pl.ds(pl.multiple_of(yh * 64, 64), 64)
    flat = norm_s[...].reshape(512, D)
    keys = dot(flat, wk_ref[...]).astype(BF16)
    vals = dot(flat, wv_ref[...]).astype(BF16)
    mine = jnp.concatenate([norm_s[k, own, :] for k in range(4)], axis=0)
    qs = dot(mine, wq_ref[...]).astype(BF16)
    a = lax.broadcasted_iota(jnp.int32, (64, 128), 0)
    b = lax.broadcasted_iota(jnp.int32, (64, 128), 1)
    lat_a = 16 * (a // 8) + 8 * yh + a % 8
    lat_b = 16 * ((b // 8) % 8) + 8 * (b // 64) + b % 8
    spread = jnp.abs(lat_a - lat_b).astype(F32) * (1.0 / 128)
    head_of = lax.broadcasted_iota(jnp.int32, (64, D), 1) // HEAD
    mixes = []
    def scored(k):
        q_one = qs[64 * k : 64 * k + 64]
        masked = jnp.concatenate([jnp.where(head_of == h, q_one, 0.0).astype(BF16) for h in range(HEADS)], axis=0)
        return lax.dot_general(
            masked, keys[128 * k : 128 * k + 128], (((1,), (1,)), ((), ())), preferred_element_type=F32
        )

    bias = jnp.concatenate([spread * table_ref[8 + h : 9 + h, :128] for h in range(HEADS)], axis=0)
    raws = [scored(k) for k in range(4)]
    expos = []
    for k in range(4):
        raw = raws[k]
        scores = bias + jnp.concatenate(
            [raw[64 * h : 64 * h + 64] * table_ref[h : h + 1, :128] for h in range(HEADS)], axis=0
        )
        expo = jnp.exp2(scores - jnp.max(scores, axis=-1, keepdims=True))
        expos.append((expo.astype(BF16), jnp.sum(expo, axis=-1, keepdims=True)))
    for k in range(4):
        expo, denom = expos[k]
        mixed = dot(expo, vals[128 * k : 128 * k + 128]) / denom
        total = jnp.where(head_of == 0, mixed[:64], 0.0)
        for h in range(1, HEADS):
            total = jnp.where(head_of == h, mixed[64 * h : 64 * h + 64], total)
        mixes.append(total.astype(BF16))
    resid = jnp.concatenate([first_s[k, own, :] for k in range(4)], axis=0)
    second = resid + dot(jnp.concatenate(mixes, axis=0), wo_ref[...])
    third = normed(second, table_ref[17:18, :])
    updated = second
    for at in range(0, 1024, 256):
        gate = dot(third, wg_ref[:, at : at + 256])
        upper = dot(third, wu_ref[:, at : at + 256])
        hidden = (gate / (1.0 + jnp.exp(-gate)) * upper).astype(BF16)
        updated = updated + dot(hidden, wd_ref[at : at + 256, :])
    for k in range(4):
        for z in range(8):
            out_ref[z, k] = updated[64 * k + 8 * z : 64 * k + 8 * z + 8].astype(BF16)


def place_kernel(x_ref, out_ref):
    to = lax.broadcasted_iota(jnp.int32, (256, 256), 0)
    source = 32 * (to % 8) + 8 * ((to // 8) % 4) + to // 32
    moves = jnp.where(lax.broadcasted_iota(jnp.int32, (256, 256), 1) == source, 1.0, 0.0).astype(BF16)
    out_ref[...] = dot(moves, x_ref[...]).astype(BF16).reshape(8, 32, D)


def key_features():
    order = np.arange(1024).reshape(YL, XA, XB, C, 32).transpose(3, 1, 0, 2, 4).reshape(1024)
    angle = order * (2.0 * math.pi / 1024)
    keyf = np.zeros((1024, 128), np.float32)
    for at, v in ((0, np.cos(angle)), (3, np.sin(angle))):
        high = v.astype(jnp.bfloat16).astype(np.float64)
        keyf[:, at], keyf[:, at + 1], keyf[:, at + 2] = high, v - high, high
    return keyf.astype(jnp.bfloat16)


def body(
    fields, norm_lon, query_lon, key_lon, value_lon, out_lon, temp_lon, bias_lon,
    norm_lat, query_lat, key_lat, value_lat, out_lat, temp_lat, bias_lat, norm_mlp, w_gate, w_up, w_down,
):
    keyf = key_features()
    twice = pl.pallas_call(
        twice_kernel,
        out_shape=jax.ShapeDtypeStruct((XA, 8, 32, D), BF16),
        in_specs=[VMEM],
        out_specs=VMEM,
        compiler_params=PARAMS,
    )(fields)
    half = lax.all_to_all(twice.reshape(16, 32, D), ("xa", "yl", "xb"), split_axis=0, concat_axis=0, tiled=True)
    row = lax.all_gather(half, "c", axis=0, tiled=True)
    row = row.reshape(1024, D)
    sent, table = pl.pallas_call(
        row_kernel,
        out_shape=(jax.ShapeDtypeStruct((2, 512, 128), BF16), jax.ShapeDtypeStruct((18, D), F32)),
        in_specs=[VMEM] * 13,
        out_specs=(VMEM, VMEM),
        scratch_shapes=[
            pltpu.VMEM((2 * HEADS, D), F32),
            pltpu.VMEM((1024, D), BF16),
            pltpu.VMEM((2, 1024, D), BF16),
            pltpu.VMEM((D, 256), F32),
            pltpu.VMEM((256, D), F32),
            pltpu.VMEM((512, 128), F32),
        ],
        compiler_params=PARAMS,
    )(
        row, norm_lon.reshape(1, D), norm_lat.reshape(1, D), norm_mlp.reshape(1, D), temp_lon.reshape(1, HEADS),
        bias_lon.reshape(1, HEADS), temp_lat.reshape(1, HEADS), bias_lat.reshape(1, HEADS), query_lon, key_lon, value_lon, out_lon, keyf,
    )
    cols = lax.all_to_all(
        sent.reshape(128, 8, 128), ("yh", "z", "yl", "xb"), split_axis=0, concat_axis=0, tiled=True
    )
    done = pl.pallas_call(
        col_kernel,
        out_shape=jax.ShapeDtypeStruct((8, 4, 8, D), BF16),
        in_specs=[VMEM] * 9,
        out_specs=VMEM,
        scratch_shapes=[
            pltpu.VMEM((1024, 128), F32),
            pltpu.VMEM((4, 128, D), F32),
            pltpu.VMEM((4, 128, D), BF16),
        ],
        compiler_params=PARAMS,
    )(
        cols.reshape(1024, 128), table, query_lat, key_lat, value_lat, out_lat, w_gate, w_up, w_down,
    )
    home = lax.all_to_all(done.reshape(8, 32, D), "z", split_axis=0, concat_axis=0, tiled=True)
    return pl.pallas_call(
        place_kernel,
        out_shape=jax.ShapeDtypeStruct((8, 32, D), BF16),
        in_specs=[VMEM],
        out_specs=VMEM,
        compiler_params=PARAMS,
    )(home.reshape(256, D))


def solution(mesh):
    fine = Mesh(mesh.devices.reshape(YL, XA, XB, C, Z, YH), ("yl", "xa", "xb", "c", "z", "yh"))
    cells = P(("z", "yh"), ("yl", "xa", "xb", "c"), None)
    return jax.shard_map(body, mesh=fine, in_specs=(cells,) + (P(),) * 18, out_specs=cells, check_vma=False)
```

```python
import functools
import math

import jax
import jax.numpy as jnp
import numpy as np
from jax import lax
from jax.experimental import pallas as pl
from jax.experimental.pallas import tpu as pltpu
from jax.sharding import Mesh
from jax.sharding import PartitionSpec as P

YL, XA, XB, C, Z, YH = 4, 2, 2, 2, 8, 2
HEADS, HEAD, D = 8, 32, 256
F32, BF16 = jnp.float32, jnp.bfloat16
LOG2E = 1.0 / math.log(2.0)
VMEM = pl.BlockSpec(memory_space=pltpu.VMEM)
PARAMS = pltpu.CompilerParams(vmem_limit_bytes=40 * 1024 * 1024)


def dot(a, b):
    return jnp.dot(a, b, preferred_element_type=F32)


def normed(values, gain):
    factor = lax.rsqrt(jnp.mean(values * values, axis=-1, keepdims=True) + 1e-06)
    return (values * factor * gain).astype(BF16)


def by_head(ref):
    at = [lax.broadcasted_iota(jnp.int32, (HEADS, HEADS), axis) for axis in range(2)]
    picked = jnp.where(at[0] == at[1], jnp.broadcast_to(ref[...], (HEADS, HEADS)), 0.0)
    return jnp.broadcast_to(jnp.sum(picked, axis=1, keepdims=True), (HEADS, D))


def row_kernel(
    x_ref, gain_ref, gain2_ref, gain3_ref, temp_ref, bias_ref, temp2_ref, bias2_ref,
    wq_ref, wk_ref, wv_ref, wo_ref, keyf_ref,
    out_ref, next_ref, table_s, norm_s, kext_s, att_s, first_s, send_s,
):
    place = 2 * lax.axis_index("c") + lax.axis_index("xa")
    own = pl.ds(pl.multiple_of(place * 256, 256), 256)
    scales = by_head(temp_ref) * (1.0 / math.sqrt(HEAD))
    table_s[:HEADS] = by_head(bias_ref) / scales
    table_s[HEADS:] = scales * LOG2E
    next_ref[0:8] = by_head(temp2_ref) * (LOG2E / math.sqrt(HEAD))
    next_ref[8:16] = by_head(bias2_ref) * LOG2E
    next_ref[16:17] = gain2_ref[...]
    next_ref[17:18] = gain3_ref[...]
    norm_s[...] = normed(x_ref[...].astype(F32), gain_ref[...])
    keys = dot(norm_s[...], wk_ref[...]).astype(BF16)
    for g in range(2):
        kext_s[g, :, :128] = keys[:, 128 * g : 128 * g + 128]
        kext_s[g, :, 128:] = keyf_ref[...]
    qs_t = dot(norm_s[own, :], wq_ref[...]).astype(BF16).T
    turned = keyf_ref[own, :].astype(F32).T
    at_row = lax.broadcasted_iota(jnp.int32, (16, 256), 0)
    wave = jnp.where(at_row < 3, turned[0:1] + turned[1:2], jnp.where(at_row < 6, turned[3:4] + turned[4:5], 0.0))
    low_rows = at_row % 3 == 2
    ones = jnp.ones((16, 1024), BF16)

    def scored(h):
        at = HEAD * (h % 4)
        full = wave * table_s[h : h + 1, :]
        high = full.astype(BF16).astype(F32)
        feats = jnp.where(low_rows, full - high, high).astype(BF16)
        parts = [qs_t[HEAD * h : HEAD * h + HEAD], feats, jnp.zeros((112, 256), BF16)]
        if at + HEAD < 128:
            parts.insert(1, jnp.zeros((128 - at - HEAD, 256), BF16))
        if at:
            parts.insert(0, jnp.zeros((at, 256), BF16))
        masked = jnp.concatenate(parts, axis=0)
        scores, peak = [], None
        for c in range(0, 1024, 512):
            scores.append(dot(kext_s[h // 4, c : c + 512, :], masked))
            for i in range(0, 512, 128):
                some = scores[-1][i : i + 128]
                peak = some if peak is None else jnp.maximum(peak, some)
        for n in (64, 32, 16, 8):
            peak = jnp.maximum(peak[:n], peak[n : 2 * n])
        return scores, jnp.max(peak, axis=0, keepdims=True)

    def mix(h, expo):
        mixed = dot(jnp.concatenate([vals_t[HEAD * h : HEAD * h + HEAD], ones], axis=0), expo)
        att_s[HEAD * h : HEAD * h + HEAD, :] = mixed[:HEAD] * (1.0 / mixed[HEAD : HEAD + 1])

    ahead, behind = scored(0), None
    vals_t = dot(norm_s[...], wv_ref[...]).astype(BF16).T
    for h in range(HEADS):
        scores, peak = ahead
        if h + 1 < HEADS:
            ahead = scored(h + 1)
        scale = table_s[8 + h : 9 + h, :]
        lift = peak * scale
        expo = jnp.concatenate([jnp.exp2(s * scale - lift).astype(BF16) for s in scores], axis=0)
        if behind is not None:
            mix(h - 1, behind)
        behind = expo
    mix(HEADS - 1, behind)
    attended = att_s[...].T.astype(BF16)
    first_s[...] = x_ref[own, :].astype(F32) + dot(attended, wo_ref[...])
    for part in range(8):
        for k in range(4):
            rows = first_s[32 * part + 8 * k : 32 * part + 8 * k + 8, :]
            send_s[pl.ds(8 * part + k, 8, stride=64), :] = rows[:, :128]
            send_s[pl.ds(8 * part + 4 + k, 8, stride=64), :] = rows[:, 128:]
    sent = send_s[...].astype(BF16)
    out_ref[0] = sent
    out_ref[1] = sent


def col_kernel(
    x_ref, table_ref, wq_ref, wk_ref, wv_ref, wo_ref, wg_ref, wu_ref, wd_ref,
    out_ref, wide_s, first_s, norm_s,
):
    wide_s[...] = x_ref[...].astype(F32)
    for k in range(4):
        for f in range(2):
            first_s[k, :, 128 * f : 128 * f + 128] = wide_s[pl.ds(4 * f + k, 128, stride=8), :]
    for k in range(4):
        norm_s[k] = normed(first_s[k], table_ref[16:17, :])
    yh = lax.axis_index("yh")
    own = pl.ds(pl.multiple_of(yh * 64, 64), 64)
    flat = norm_s[...].reshape(512, D)
    keys = dot(flat, wk_ref[...]).astype(BF16)
    vals = dot(flat, wv_ref[...]).astype(BF16)
    mine = jnp.concatenate([norm_s[k, own, :] for k in range(4)], axis=0)
    qs = dot(mine, wq_ref[...]).astype(BF16)
    a = lax.broadcasted_iota(jnp.int32, (64, 128), 0)
    b = lax.broadcasted_iota(jnp.int32, (64, 128), 1)
    lat_a = 16 * (a // 8) + 8 * yh + a % 8
    lat_b = 16 * ((b // 8) % 8) + 8 * (b // 64) + b % 8
    spread = jnp.abs(lat_a - lat_b).astype(F32) * (1.0 / 128)
    head_of = lax.broadcasted_iota(jnp.int32, (64, D), 1) // HEAD
    mixes = []
    def scored(k):
        q_one = qs[64 * k : 64 * k + 64]
        masked = jnp.concatenate([jnp.where(head_of == h, q_one, 0.0).astype(BF16) for h in range(HEADS)], axis=0)
        return lax.dot_general(
            masked, keys[128 * k : 128 * k + 128], (((1,), (1,)), ((), ())), preferred_element_type=F32
        )

    bias = jnp.concatenate([spread * table_ref[8 + h : 9 + h, :128] for h in range(HEADS)], axis=0)
    raws = [scored(k) for k in range(4)]
    expos = []
    for k in range(4):
        raw = raws[k]
        scores = bias + jnp.concatenate(
            [raw[64 * h : 64 * h + 64] * table_ref[h : h + 1, :128] for h in range(HEADS)], axis=0
        )
        expo = jnp.exp2(scores - jnp.max(scores, axis=-1, keepdims=True))
        expos.append((expo.astype(BF16), jnp.sum(expo, axis=-1, keepdims=True)))
    for k in range(4):
        expo, denom = expos[k]
        mixed = dot(expo, vals[128 * k : 128 * k + 128]) / denom
        total = jnp.where(head_of == 0, mixed[:64], 0.0)
        for h in range(1, HEADS):
            total = jnp.where(head_of == h, mixed[64 * h : 64 * h + 64], total)
        mixes.append(total.astype(BF16))
    resid = jnp.concatenate([first_s[k, own, :] for k in range(4)], axis=0)
    second = resid + dot(jnp.concatenate(mixes, axis=0), wo_ref[...])
    third = normed(second, table_ref[17:18, :])
    updated = second
    for at in range(0, 1024, 256):
        gate = dot(third, wg_ref[:, at : at + 256])
        upper = dot(third, wu_ref[:, at : at + 256])
        hidden = (gate / (1.0 + jnp.exp(-gate)) * upper).astype(BF16)
        updated = updated + dot(hidden, wd_ref[at : at + 256, :])
    for k in range(4):
        for z in range(8):
            out_ref[z, k] = updated[64 * k + 8 * z : 64 * k + 8 * z + 8].astype(BF16)


def place_kernel(x_ref, out_ref):
    to = lax.broadcasted_iota(jnp.int32, (256, 256), 0)
    source = 32 * (to % 8) + 8 * ((to // 8) % 4) + to // 32
    moves = jnp.where(lax.broadcasted_iota(jnp.int32, (256, 256), 1) == source, 1.0, 0.0).astype(BF16)
    out_ref[...] = dot(moves, x_ref[...]).astype(BF16).reshape(8, 32, D)


def key_features():
    order = np.arange(1024).reshape(YL, XA, XB, C, 32).transpose(3, 1, 0, 2, 4).reshape(1024)
    angle = order * (2.0 * math.pi / 1024)
    keyf = np.zeros((1024, 128), np.float32)
    for at, v in ((0, np.cos(angle)), (3, np.sin(angle))):
        high = v.astype(jnp.bfloat16).astype(np.float64)
        keyf[:, at], keyf[:, at + 1], keyf[:, at + 2] = high, v - high, high
    return keyf.astype(jnp.bfloat16)


def body(
    fields, norm_lon, query_lon, key_lon, value_lon, out_lon, temp_lon, bias_lon,
    norm_lat, query_lat, key_lat, value_lat, out_lat, temp_lat, bias_lat, norm_mlp, w_gate, w_up, w_down,
):
    keyf = key_features()
    twice = jnp.concatenate([fields] * XA, axis=0)
    half = lax.all_to_all(twice.reshape(16, 32, D), ("xa", "yl", "xb"), split_axis=0, concat_axis=0, tiled=True)
    row = lax.all_gather(half, "c", axis=0, tiled=True)
    row = row.reshape(1024, D)
    sent, table = pl.pallas_call(
        row_kernel,
        out_shape=(jax.ShapeDtypeStruct((2, 512, 128), BF16), jax.ShapeDtypeStruct((18, D), F32)),
        in_specs=[VMEM] * 13,
        out_specs=(VMEM, VMEM),
        scratch_shapes=[
            pltpu.VMEM((2 * HEADS, D), F32),
            pltpu.VMEM((1024, D), BF16),
            pltpu.VMEM((2, 1024, D), BF16),
            pltpu.VMEM((D, 256), F32),
            pltpu.VMEM((256, D), F32),
            pltpu.VMEM((512, 128), F32),
        ],
        compiler_params=PARAMS,
    )(
        row, norm_lon.reshape(1, D), norm_lat.reshape(1, D), norm_mlp.reshape(1, D), temp_lon.reshape(1, HEADS),
        bias_lon.reshape(1, HEADS), temp_lat.reshape(1, HEADS), bias_lat.reshape(1, HEADS), query_lon, key_lon, value_lon, out_lon, keyf,
    )
    cols = lax.all_to_all(
        sent.reshape(128, 8, 128), ("yh", "z", "yl", "xb"), split_axis=0, concat_axis=0, tiled=True
    )
    done = pl.pallas_call(
        col_kernel,
        out_shape=jax.ShapeDtypeStruct((8, 4, 8, D), BF16),
        in_specs=[VMEM] * 9,
        out_specs=VMEM,
        scratch_shapes=[
            pltpu.VMEM((1024, 128), F32),
            pltpu.VMEM((4, 128, D), F32),
            pltpu.VMEM((4, 128, D), BF16),
        ],
        compiler_params=PARAMS,
    )(
        cols.reshape(1024, 128), table, query_lat, key_lat, value_lat, out_lat, w_gate, w_up, w_down,
    )
    home = lax.all_to_all(done.reshape(8, 32, D), "z", split_axis=0, concat_axis=0, tiled=True)
    return pl.pallas_call(
        place_kernel,
        out_shape=jax.ShapeDtypeStruct((8, 32, D), BF16),
        in_specs=[VMEM],
        out_specs=VMEM,
        compiler_params=PARAMS,
    )(home.reshape(256, D))


def solution(mesh):
    fine = Mesh(mesh.devices.reshape(YL, XA, XB, C, Z, YH), ("yl", "xa", "xb", "c", "z", "yh"))
    cells = P(("z", "yh"), ("yl", "xa", "xb", "c"), None)
    return jax.shard_map(body, mesh=fine, in_specs=(cells,) + (P(),) * 18, out_specs=cells, check_vma=False)
```
